256 devices in a mesh: tm: 8 (over x, y_hi), rows: 32 (over z, y_lo, core).
Axes of the slice: x: 4, y: 4 (y_hi: 2, y_lo: 2; y = y_hi * 2 + y_lo), z: 8, core: 2. Of those that a mesh axis runs over, the one named last changes fastest.
Arguments:
- queries: bfloat16 [16, 64, 96, 1024], P('tm', 'rows'), may hold values from -5 to 5
- keys: bfloat16 [16, 64, 96, 1024], P('tm', 'rows'), may hold values from -5 to 5
- values: bfloat16 [16, 64, 96, 1024], P('tm', 'rows'), may hold values from -5 to 5
- window_lists: int32 [256, 12], replicated, may hold values from -1 to 255, as said below
Outputs:
- attended: bfloat16 [16, 64, 96, 1024], P('tm', 'rows')
The draws below stay inside these ranges and needn't reach their ends.
Inputs may be any that keep to these rules, and one draw needn't show every extreme that they name: `window_lists`: each row lists distinct tiles whose frame-tile, row-tile and column-tile indices each differ from the row's own tile by at most one; the tile itself is always listed; listed ids come first, then -1; some row lists 12 tiles.
All inputs are finite; a program needn't handle non-finite values.
Results may differ from the reference program's by a relative error of at most 0.0047.
Values may be sent and summed in bfloat16 or wider, within the bound.
A program may use at most 64 MiB of HBM per device.

```python
import jax
import jax.numpy as jnp
from jax import lax

HEAD_DIM = 128
HEADS = 8
TILE_T = 2
TILE_H = 8
TILE_W = 24
WIN = 12
TILE_COLS = 4
FRAMES = 16
HEIGHT = 64
WIDTH = 96
FEAT = 1024
TILE_ROWS = 8
TILES = 256
TOK_TILE = 384
N_TM = 8


def draw_queries(key, part):
    key = jax.random.fold_in(key, 5)
    shape = (FRAMES, HEIGHT, WIDTH, HEADS, HEAD_DIM)
    field = jnp.clip(jax.random.normal(key, shape), -5.0, 5.0)
    return field.reshape(FRAMES, HEIGHT, WIDTH, FEAT).astype(jnp.bfloat16)


def draw_keys(key, part):
    key = jax.random.fold_in(key, 7)
    shape = (FRAMES, HEIGHT, WIDTH, HEADS, HEAD_DIM)
    field = jnp.clip(jax.random.normal(key, shape), -5.0, 5.0)
    return field.reshape(FRAMES, HEIGHT, WIDTH, FEAT).astype(jnp.bfloat16)


def draw_window_lists(key, part):
    key = jax.random.fold_in(key, 11)
    prio_key, want_key = jax.random.split(key)
    tile = jnp.arange(TILES, dtype=jnp.int32)
    per_layer = TILE_ROWS * TILE_COLS
    layer = tile // per_layer
    row_tile = tile // TILE_COLS % TILE_ROWS
    col_tile = tile % TILE_COLS
    offset = jnp.arange(27, dtype=jnp.int32)
    layer_step = offset // 9 - 1
    row_step = offset // 3 % 3 - 1
    col_step = offset % 3 - 1
    near_layer = layer[:, None] + layer_step[None, :]
    near_row = row_tile[:, None] + row_step[None, :]
    near_col = col_tile[:, None] + col_step[None, :]
    inside = (near_layer >= 0) & (near_layer < N_TM) & (near_row >= 0) & (near_row < TILE_ROWS) & (near_col >= 0) & (near_col < TILE_COLS)
    near_id = (near_layer * TILE_ROWS + near_row) * TILE_COLS + near_col
    prio = jax.random.randint(prio_key, (TILES, 27), 0, 1000)
    prio = jnp.where(offset[None, :] == 13, 2000, prio)
    prio = jnp.where(inside, prio, -1)
    ranking = prio * 32 + offset[None, :]
    order = jnp.argsort(-ranking, axis=1)
    chosen = jnp.take_along_axis(near_id, order, axis=1)[:, :WIN]
    inside_count = jnp.sum(inside.astype(jnp.int32), axis=1)
    wanted = jax.random.randint(want_key, (TILES,), WIN // 2, 2 * WIN)
    wanted = jnp.where(tile == per_layer, WIN, wanted)
    keep_count = jnp.minimum(wanted, inside_count)
    slots = jnp.arange(WIN, dtype=jnp.int32)
    return jnp.where(slots[None, :] < keep_count[:, None], chosen, -1).astype(jnp.int32)


def steps_of(own_key, dims, cuts, least, largest):
    gain = 1.0
    for position, shards_of in cuts:
        heights = jax.random.uniform(jax.random.fold_in(jax.random.fold_in(own_key, 6), position), (shards_of,), jnp.float32, least / len(cuts), largest / len(cuts))
        gain = gain * jnp.repeat(jnp.exp(heights), dims[position] // shards_of).reshape((-1,) + (1,) * (len(dims) - 1 - position))
    return gain


def gaussian(own_key, dims, deviation, limit, pieces=(), held_as=jnp.bfloat16):
    drawn = jax.random.normal(own_key, dims, jnp.float32) * deviation
    if len(pieces) > 0:
        drawn = steps_of(own_key, dims, pieces, -0.22, 0.18) * drawn
    return jnp.clip(drawn, min=-limit, max=limit).astype(held_as)


def setup_inputs(seed: int = 0) -> dict:
    streams_of = jax.random.split(jax.random.key(seed), 5)
    return {
        "queries": draw_queries(jax.random.fold_in(streams_of[4], 71), 0),
        "keys": draw_keys(jax.random.fold_in(streams_of[4], 71), 0),
        "values": gaussian(streams_of[2], (FRAMES, HEIGHT, WIDTH, FEAT), 1.0, 5.0, ((0, 8), (1, 32))),
        "window_lists": draw_window_lists(jax.random.fold_in(streams_of[4], 71), 0),
    }


def to_tiles(field):
    chans = field.shape[-1]
    tiles = field.reshape(N_TM, TILE_T, TILE_ROWS, TILE_H, TILE_COLS, TILE_W, chans)
    tiles = jnp.transpose(tiles, (0, 2, 4, 1, 3, 5, 6))
    return tiles.reshape(TILES, TOK_TILE, chans)


def reference(queries, keys, values, window_lists):
    query_tiles = to_tiles(queries).reshape(TILES, TOK_TILE, HEADS, HEAD_DIM)
    key_tiles = to_tiles(keys).reshape(TILES, TOK_TILE, HEADS, HEAD_DIM)
    value_tiles = to_tiles(values).reshape(TILES, TOK_TILE, HEADS, HEAD_DIM)
    scale = HEAD_DIM ** -0.5

    def attend(inputs):
        query_tile, listed = inputs
        present = listed >= 0
        picked = jnp.where(present, listed, 0).astype(jnp.int32)
        key_rows = jnp.take(key_tiles, picked, axis=0).reshape(WIN * TOK_TILE, HEADS, HEAD_DIM).astype(jnp.float32)
        value_rows = jnp.take(value_tiles, picked, axis=0).reshape(WIN * TOK_TILE, HEADS, HEAD_DIM).astype(jnp.float32)
        scores = jnp.einsum("qhd,khd->hqk", query_tile.astype(jnp.float32), key_rows) * scale
        allowed = jnp.repeat(present, TOK_TILE)
        scores = jnp.where(allowed[None, None, :], scores, -1e30)
        peak = jnp.max(scores, axis=2, keepdims=True)
        weights = jnp.exp(scores - peak)
        total = jnp.sum(weights, axis=2, keepdims=True)
        rounded = lax.optimization_barrier(weights.astype(jnp.bfloat16)).astype(jnp.float32)
        mixed = jnp.einsum("hqk,khd->qhd", rounded, value_rows)
        return (mixed / jnp.transpose(total, (1, 0, 2))).astype(jnp.bfloat16)

    result = lax.map(attend, (query_tiles, window_lists))
    result = result.reshape(N_TM, TILE_ROWS, TILE_COLS, TILE_T, TILE_H, TILE_W, FEAT)
    result = jnp.transpose(result, (0, 3, 1, 4, 2, 5, 6))
    return result.reshape(FRAMES, HEIGHT, WIDTH, FEAT)
```

```python
import functools

import jax
import jax.numpy as jnp
from jax import lax
from jax.experimental import pallas as pl
from jax.experimental.pallas import tpu as pltpu
from jax.sharding import PartitionSpec as P

HEADS = 8
COLS = 4
WIN = 12
TOK = 384
PART = 96
DIM = 128
LOG2E = 1.4426950408889634


def rc(src, dst, ss, rs, dev):
    return pltpu.make_async_remote_copy(
        src_ref=src, dst_ref=dst, send_sem=ss, recv_sem=rs, device_id=dev, device_id_type=pl.DeviceIdType.MESH
    )


def kernel(
    n_tm, n_rows, q_hbm, k_hbm, v_hbm, lists, out_hbm,
    qin, kin, vin, skv, sq, kv, qb, scores, ob, orecv, outv,
    in_sem, out_sem, kv_send, kv_recv, q_send, q_recv, z_send, z_recv, x_send, x_recv, o_send, o_recv, loc_sem,
):
    tm = lax.axis_index("tm")
    rows = lax.axis_index("rows")
    x, yh = tm // 2, tm % 2
    z, part = rows // 4, rows % 4
    me = yh * 4 + part

    def member(p):
        return (x * 2 + p // 4, z * 4 + p % 4)

    z_up = (tm, (rows + 4) % n_rows)
    z_dn = (tm, (rows + n_rows - 4) % n_rows)
    x_up = ((tm + 2) % n_tm, rows)
    x_dn = ((tm + n_tm - 2) % n_tm, rows)

    loads = [
        pltpu.make_async_copy(src, dst, in_sem.at[i])
        for i, (src, dst) in enumerate(((k_hbm, kin), (v_hbm, vin), (q_hbm, qin)))
    ]
    for c in loads:
        c.start()

    barrier = pltpu.get_barrier_semaphore()

    def greet(d, carry):
        pl.semaphore_signal(barrier, inc=1, device_id=member((me + d) % 8), device_id_type=pl.DeviceIdType.MESH)
        return carry

    lax.fori_loop(1, 8, greet, 0)
    for dev in (z_up, z_dn, x_up, x_dn):
        pl.semaphore_signal(barrier, inc=1, device_id=dev, device_id_type=pl.DeviceIdType.MESH)
    pl.semaphore_wait(barrier, 11)

    def pack(src, ct, p):
        feats = pl.ds(pl.multiple_of(p * DIM, DIM), DIM)
        pieces = []
        for f in range(2):
            for r in range(2):
                full = src[f, r, :, feats].astype(jnp.float32)
                pieces.append(full[ct * 24 : ct * 24 + 24])
        return jnp.concatenate(pieces, axis=0).astype(jnp.bfloat16)

    my_rows = pl.ds(pl.multiple_of(part * PART, PART), PART)

    def kv_piece(ct, d):
        p = (me + d) % 8
        return rc(
            skv.at[p, ct], kv.at[ct, 1 + yh, 1, :, my_rows], kv_send.at[ct, p], kv_recv.at[ct, me], member(p)
        )

    def kv_arrival(ct, p):
        return rc(
            skv.at[p, ct],
            kv.at[ct, 1 + p // 4, 1, :, pl.ds(pl.multiple_of((p % 4) * PART, PART), PART)],
            kv_send.at[ct, p], kv_recv.at[ct, p], member(p),
        )

    def q_piece(d):
        p = (me + d) % 8
        return rc(sq.at[p], qb.at[yh, :, my_rows], q_send.at[p], q_recv.at[me], member(p))

    def q_arrival(p):
        return rc(
            sq.at[p], qb.at[p // 4, :, pl.ds(pl.multiple_of((p % 4) * PART, PART), PART)],
            q_send.at[p], q_recv.at[p], member(p),
        )

    loads[0].wait()
    loads[1].wait()
    own_copies = []
    for ct in range(COLS):
        def send_kv(d, carry, ct=ct):
            p = (me + d) % 8
            skv[p, ct, 0] = pack(kin, ct, p)
            skv[p, ct, 1] = pack(vin, ct, p)
            kv_piece(ct, d).start()
            return carry

        lax.fori_loop(1, 8, send_kv, 0)
        skv[me, ct, 0] = pack(kin, ct, me)
        skv[me, ct, 1] = pack(vin, ct, me)
        own = pltpu.make_async_copy(skv.at[me, ct], kv.at[ct, 1 + yh, 1, :, my_rows], loc_sem.at[ct])
        own.start()
        own_copies.append(own)
    loads[2].wait()

    def send_q(d, carry):
        p = (me + d) % 8
        for ct in range(COLS):
            sq[p, ct] = pack(qin, ct, p)
        q_piece(d).start()
        return carry

    lax.fori_loop(1, 8, send_q, 0)
    for ct in range(COLS):
        sq[me, ct] = pack(qin, ct, me)
    own_q = pltpu.make_async_copy(sq.at[me], qb.at[yh, :, my_rows], loc_sem.at[COLS])
    own_q.start()

    def z_copy(ct, up, layer):
        dev = z_up if up else z_dn
        return rc(
            kv.at[ct, layer, 1], kv.at[ct, layer, 0 if up else 2],
            z_send.at[ct, up, layer], z_recv.at[ct, up, layer], dev,
        )

    def x_copy(ct, up, row):
        dev = x_up if up else x_dn
        return rc(
            kv.at[ct, 2 if up else 1, row], kv.at[ct, 0 if up else 3, row],
            x_send.at[ct, up, row], x_recv.at[ct, up, row], dev,
        )

    started = []

    def begin(c):
        c.start()
        started.append(c)

    for ct in range(COLS):
        own_copies[ct].wait()

        def take(d, carry, ct=ct):
            kv_arrival(ct, (me + d) % 8).wait_recv()
            return carry

        lax.fori_loop(1, 8, take, 0)
        for up in (1, 0):
            for layer in (1, 2):
                begin(z_copy(ct, up, layer))
            begin(x_copy(ct, up, 1))
    for ct in range(COLS):
        if ct < COLS - 1:
            for up in (1, 0):
                for layer in (1, 2):
                    z_copy(ct, up, layer).wait_recv()
            for up in (1, 0):
                for row in (0, 2):
                    begin(x_copy(ct, up, row))
        else:
            for up in (1, 0):
                x_copy(ct, up, 1).wait_recv()
            for up in (1, 0):
                for layer in (0, 3):
                    begin(z_copy(ct, up, layer))
    for ct in range(COLS):
        for up in (1, 0):
            if ct < COLS - 1:
                for row in (0, 1, 2):
                    x_copy(ct, up, row).wait_recv()
            else:
                for layer in (0, 1, 2, 3):
                    z_copy(ct, up, layer).wait_recv()
    own_q.wait()

    def take_q(d, carry):
        q_arrival((me + d) % 8).wait_recv()
        return carry

    lax.fori_loop(1, 8, take_q, 0)

    scale = DIM ** -0.5 * LOG2E
    ones = jnp.ones((TOK, DIM), jnp.bfloat16)

    def o_piece(i, s):
        layer, ct = i % 2, i // 2
        p = layer * 4 + s
        return rc(
            ob.at[layer, ct, pl.ds(s * PART, PART)], orecv.at[me, ct], o_send.at[i, s], o_recv.at[me, ct], member(p)
        )

    def own_o(ct):
        return pltpu.make_async_copy(ob.at[yh, ct, my_rows], orecv.at[me, ct], loc_sem.at[COLS + 1 + ct])

    def attend(i, carry):
        layer, ct = i % 2, i // 2
        tile = ((2 * x + layer) * 8 + z) * COLS + ct

        def place(slot):
            listed = lists[tile * WIN + slot]
            present = listed >= 0
            t = jnp.where(present, listed, tile)
            t_layer, t_row, t_col = t // 32, (t // 4) % 8, t % 4
            return t_col, jnp.clip(t_layer - 2 * x + 1, 0, 3), jnp.clip(t_row - z + 1, 0, 2), jnp.where(present, 1.0, 0.0)

        q = qb[layer, ct]
        peak = jnp.full((TOK, DIM), -jnp.inf, jnp.float32)
        for j in range(WIN // 2):
            keys = []
            for slot in (2 * j, 2 * j + 1):
                c_, l_, r_, _ = place(slot)
                keys.append(kv[c_, l_, r_, 0])
            s = lax.dot_general(
                q, jnp.concatenate(keys, axis=0), (((1,), (1,)), ((), ())), preferred_element_type=jnp.float32
            )
            scores[:, j * 2 * TOK : (j + 1) * 2 * TOK] = s
            for b in range(2 * TOK // DIM):
                peak = jnp.maximum(peak, s[:, b * DIM : (b + 1) * DIM])
        top = jnp.max(peak, axis=1, keepdims=True) * scale
        acc = jnp.zeros((TOK, 2 * DIM), jnp.float32)
        for j in range(WIN // 2):
            vals = []
            for slot in (2 * j, 2 * j + 1):
                c_, l_, r_, flag = place(slot)
                flag = jnp.full((TOK, DIM), flag, jnp.float32).astype(jnp.bfloat16)
                vals.append(jnp.concatenate((kv[c_, l_, r_, 1] * flag, ones * flag), axis=1))
            w = jnp.exp2(scores[:, j * 2 * TOK : (j + 1) * 2 * TOK] * scale - top).astype(jnp.bfloat16)
            acc = acc + jnp.dot(w, jnp.concatenate(vals, axis=0), preferred_element_type=jnp.float32)
        ob[layer, ct] = (acc[:, :DIM] / acc[:, DIM:]).astype(jnp.bfloat16)
        return carry

    def finish(i, carry):
        attend(i, carry)
        layer, ct = i % 2, i // 2
        for s in range(4):
            @pl.when(layer * 4 + s != me)
            def _():
                o_piece(i, s).start()

        @pl.when(layer == yh)
        def _():
            own_o(ct).start()

        return carry

    lax.fori_loop(0, 8, finish, 0)

    def drain(ct, carry):
        own_o(ct).wait()

        def take_o(d, c):
            p = (me + d) % 8
            rc(ob.at[yh, ct, my_rows], orecv.at[p, ct], o_send.at[0, 0], o_recv.at[p, ct], member(p)).wait_recv()
            return c

        lax.fori_loop(1, 8, take_o, 0)
        return carry

    lax.fori_loop(0, COLS, drain, 0)

    for h in range(HEADS):
        parts = [orecv[h, ct].astype(jnp.float32) for ct in range(COLS)]
        for f in range(2):
            for r in range(2):
                n = (2 * f + r) * 24
                row = jnp.concatenate([p_[n : n + 24] for p_ in parts], axis=0)
                outv[f, r, :, h * DIM : (h + 1) * DIM] = row.astype(jnp.bfloat16)
    done = pltpu.make_async_copy(outv, out_hbm, out_sem)
    done.start()

    def sent(d, carry):
        p = (me + d) % 8
        for ct in range(COLS):
            kv_piece(ct, d).wait_send()
        q_piece(d).wait_send()
        return carry

    lax.fori_loop(1, 8, sent, 0)
    for c in started:
        c.wait_send()

    def sent_o(i, carry):
        for s in range(4):
            @pl.when((i % 2) * 4 + s != me)
            def _():
                o_piece(i, s).wait_send()
        return carry

    lax.fori_loop(0, 8, sent_o, 0)
    done.wait()


def solution(mesh):
    n_tm, n_rows = mesh.shape["tm"], mesh.shape["rows"]
    bf = jnp.bfloat16
    vm = pltpu.VMEM
    dma = pltpu.SemaphoreType.DMA

    def body(queries, keys, values, window_lists):
        any_ = pl.BlockSpec(memory_space=pl.ANY)
        return pl.pallas_call(
            functools.partial(kernel, n_tm, n_rows),
            out_shape=jax.ShapeDtypeStruct(queries.shape, bf),
            in_specs=[any_, any_, any_, pl.BlockSpec(memory_space=pltpu.SMEM)],
            out_specs=any_,
            scratch_shapes=[
                vm(queries.shape, bf), vm(queries.shape, bf), vm(queries.shape, bf),
                vm((HEADS, COLS, 2, PART, DIM), bf),
                vm((HEADS, COLS, PART, DIM), bf),
                vm((COLS, 4, 3, 2, TOK, DIM), bf),
                vm((2, COLS, TOK, DIM), bf),
                vm((TOK, WIN * TOK), jnp.float32),
                vm((2, COLS, TOK, DIM), bf),
                vm((HEADS, COLS, PART, DIM), bf),
                vm(queries.shape, bf),
                dma((3,)), dma, dma((COLS, 8)), dma((COLS, 8)), dma((8,)), dma((8,)),
                dma((COLS, 2, 4)), dma((COLS, 2, 4)), dma((COLS, 2, 3)), dma((COLS, 2, 3)),
                dma((8, 4)), dma((8, COLS)), dma((2 * COLS + 1,)),
            ],
            compiler_params=pltpu.CompilerParams(
                collective_id=0, has_side_effects=True, vmem_limit_bytes=56 * 1024 * 1024
            ),
        )(queries, keys, values, window_lists.reshape(-1))

    row = P("tm", "rows", None, None)
    return jax.shard_map(body, mesh=mesh, in_specs=(row, row, row, P()), out_specs=row, check_vma=False)
```

```python
import functools

import jax
import jax.numpy as jnp
from jax import lax
from jax.experimental import pallas as pl
from jax.experimental.pallas import tpu as pltpu
from jax.sharding import PartitionSpec as P

HEADS = 8
COLS = 4
WIN = 12
TOK = 384
PART = 96
DIM = 128
LOG2E = 1.4426950408889634


def rc(src, dst, ss, rs, dev):
    return pltpu.make_async_remote_copy(
        src_ref=src, dst_ref=dst, send_sem=ss, recv_sem=rs, device_id=dev, device_id_type=pl.DeviceIdType.MESH
    )


def kernel(
    n_tm, n_rows, q_hbm, k_hbm, v_hbm, lists, out_hbm,
    qin, kin, vin, skv, sq, kv, qb, scores, peak, ob, orecv, outv,
    in_sem, out_sem, kv_send, kv_recv, q_send, q_recv, z_send, z_recv, x_send, x_recv, o_send, o_recv, loc_sem,
):
    tm = lax.axis_index("tm")
    rows = lax.axis_index("rows")
    x, yh = tm // 2, tm % 2
    z, part = rows // 4, rows % 4
    me = yh * 4 + part

    def member(p):
        return (x * 2 + p // 4, z * 4 + p % 4)

    z_up = (tm, (rows + 4) % n_rows)
    z_dn = (tm, (rows + n_rows - 4) % n_rows)
    x_up = ((tm + 2) % n_tm, rows)
    x_dn = ((tm + n_tm - 2) % n_tm, rows)

    loads = [
        pltpu.make_async_copy(src, dst, in_sem.at[i])
        for i, (src, dst) in enumerate(((k_hbm, kin), (v_hbm, vin), (q_hbm, qin)))
    ]
    for c in loads:
        c.start()

    barrier = pltpu.get_barrier_semaphore()

    def greet(d, carry):
        pl.semaphore_signal(barrier, inc=1, device_id=member((me + d) % 8), device_id_type=pl.DeviceIdType.MESH)
        return carry

    lax.fori_loop(1, 8, greet, 0)
    for dev in (z_up, z_dn, x_up, x_dn):
        pl.semaphore_signal(barrier, inc=1, device_id=dev, device_id_type=pl.DeviceIdType.MESH)
    pl.semaphore_wait(barrier, 11)

    def pack(src, ct, p):
        feats = pl.ds(pl.multiple_of(p * DIM, DIM), DIM)
        pieces = []
        for f in range(2):
            for r in range(2):
                full = src[f, r, :, feats].astype(jnp.float32)
                pieces.append(full[ct * 24 : ct * 24 + 24])
        return jnp.concatenate(pieces, axis=0).astype(jnp.bfloat16)

    my_rows = pl.ds(pl.multiple_of(part * PART, PART), PART)

    def kv_piece(ct, d):
        p = (me + d) % 8
        return rc(
            skv.at[p, ct], kv.at[ct, 1 + yh, 1, :, my_rows], kv_send.at[ct, p], kv_recv.at[ct, me], member(p)
        )

    def kv_arrival(ct, p):
        return rc(
            skv.at[p, ct],
            kv.at[ct, 1 + p // 4, 1, :, pl.ds(pl.multiple_of((p % 4) * PART, PART), PART)],
            kv_send.at[ct, p], kv_recv.at[ct, p], member(p),
        )

    def q_piece(d):
        p = (me + d) % 8
        return rc(sq.at[p], qb.at[yh, :, my_rows], q_send.at[p], q_recv.at[me], member(p))

    def q_arrival(p):
        return rc(
            sq.at[p], qb.at[p // 4, :, pl.ds(pl.multiple_of((p % 4) * PART, PART), PART)],
            q_send.at[p], q_recv.at[p], member(p),
        )

    loads[0].wait()
    loads[1].wait()
    own_copies = []
    for ct in range(COLS):
        def send_kv(d, carry, ct=ct):
            p = (me + d) % 8
            skv[p, ct, 0] = pack(kin, ct, p)
            skv[p, ct, 1] = pack(vin, ct, p)
            kv_piece(ct, d).start()
            return carry

        lax.fori_loop(1, 8, send_kv, 0)
        skv[me, ct, 0] = pack(kin, ct, me)
        skv[me, ct, 1] = pack(vin, ct, me)
        own = pltpu.make_async_copy(skv.at[me, ct], kv.at[ct, 1 + yh, 1, :, my_rows], loc_sem.at[ct])
        own.start()
        own_copies.append(own)
    loads[2].wait()

    def send_q(d, carry):
        p = (me + d) % 8
        for ct in range(COLS):
            sq[p, ct] = pack(qin, ct, p)
        q_piece(d).start()
        return carry

    lax.fori_loop(1, 8, send_q, 0)
    for ct in range(COLS):
        sq[me, ct] = pack(qin, ct, me)
    own_q = pltpu.make_async_copy(sq.at[me], qb.at[yh, :, my_rows], loc_sem.at[COLS])
    own_q.start()

    def z_copy(ct, up, layer):
        dev = z_up if up else z_dn
        return rc(
            kv.at[ct, layer, 1], kv.at[ct, layer, 0 if up else 2],
            z_send.at[ct, up, layer], z_recv.at[ct, up, layer], dev,
        )

    def x_copy(ct, up, row):
        dev = x_up if up else x_dn
        return rc(
            kv.at[ct, 2 if up else 1, row], kv.at[ct, 0 if up else 3, row],
            x_send.at[ct, up, row], x_recv.at[ct, up, row], dev,
        )

    started = []

    def begin(c):
        c.start()
        started.append(c)

    for ct in range(COLS):
        own_copies[ct].wait()

        def take(d, carry, ct=ct):
            kv_arrival(ct, (me + d) % 8).wait_recv()
            return carry

        lax.fori_loop(1, 8, take, 0)
        for up in (1, 0):
            for layer in (1, 2):
                begin(z_copy(ct, up, layer))
            begin(x_copy(ct, up, 1))
    for ct in range(COLS):
        if ct < COLS - 1:
            for up in (1, 0):
                for layer in (1, 2):
                    z_copy(ct, up, layer).wait_recv()
            for up in (1, 0):
                for row in (0, 2):
                    begin(x_copy(ct, up, row))
        else:
            for up in (1, 0):
                x_copy(ct, up, 1).wait_recv()
            for up in (1, 0):
                for layer in (0, 3):
                    begin(z_copy(ct, up, layer))
    for ct in range(COLS):
        for up in (1, 0):
            if ct < COLS - 1:
                for row in (0, 1, 2):
                    x_copy(ct, up, row).wait_recv()
            else:
                for layer in (0, 1, 2, 3):
                    z_copy(ct, up, layer).wait_recv()
    own_q.wait()

    def take_q(d, carry):
        q_arrival((me + d) % 8).wait_recv()
        return carry

    lax.fori_loop(1, 8, take_q, 0)

    scale = DIM ** -0.5 * LOG2E

    def o_piece(i, s):
        layer, ct = i % 2, i // 2
        p = layer * 4 + s
        return rc(
            ob.at[layer, ct, pl.ds(s * PART, PART)], orecv.at[me, ct], o_send.at[i, s], o_recv.at[me, ct], member(p)
        )

    def own_o(ct):
        return pltpu.make_async_copy(ob.at[yh, ct, my_rows], orecv.at[me, ct], loc_sem.at[COLS + 1 + ct])

    def attend(i, carry):
        layer, ct = i % 2, i // 2
        tile = ((2 * x + layer) * 8 + z) * COLS + ct

        def place(slot):
            listed = lists[tile * WIN + slot]
            present = listed >= 0
            t = jnp.where(present, listed, tile)
            t_layer, t_row, t_col = t // 32, (t // 4) % 8, t % 4
            return t_col, jnp.clip(t_layer - 2 * x + 1, 0, 3), jnp.clip(t_row - z + 1, 0, 2), jnp.where(present, 1.0, 0.0)

        @pl.when(tm >= 0)
        def _():
            q = qb[layer, ct]
            high = jnp.full((TOK, DIM), -jnp.inf, jnp.float32)
            for j in range(WIN // 2):
                keys = []
                for slot in (2 * j, 2 * j + 1):
                    c_, l_, r_, _ = place(slot)
                    keys.append(kv[c_, l_, r_, 0])
                s = lax.dot_general(
                    q, jnp.concatenate(keys, axis=0), (((1,), (1,)), ((), ())), preferred_element_type=jnp.float32
                )
                scores[j] = s
                for b in range(2 * TOK // DIM):
                    high = jnp.maximum(high, s[:, b * DIM : (b + 1) * DIM])
            peak[...] = jnp.broadcast_to(jnp.max(high, axis=1, keepdims=True) * scale, (TOK, DIM))

        @pl.when(rows >= 0)
        def _():
            top = jnp.concatenate([peak[...]] * (2 * TOK // DIM), axis=1)
            acc = jnp.zeros((TOK, 2 * DIM), jnp.float32)
            for j in range(WIN // 2):
                vals = []
                for slot in (2 * j, 2 * j + 1):
                    c_, l_, r_, flag = place(slot)
                    flag = jnp.full((TOK, DIM), flag, jnp.float32).astype(jnp.bfloat16)
                    vals.append(jnp.concatenate((kv[c_, l_, r_, 1] * flag, flag), axis=1))
                w = jnp.exp2(scores[j] * scale - top).astype(jnp.bfloat16)
                acc = acc + jnp.dot(w, jnp.concatenate(vals, axis=0), preferred_element_type=jnp.float32)
            ob[layer, ct] = (acc[:, :DIM] / acc[:, DIM:]).astype(jnp.bfloat16)

        return carry

    def finish(i, carry):
        attend(i, carry)
        layer, ct = i % 2, i // 2
        for s in range(4):
            @pl.when(layer * 4 + s != me)
            def _():
                o_piece(i, s).start()

        @pl.when(layer == yh)
        def _():
            own_o(ct).start()

        return carry

    lax.fori_loop(0, 8, finish, 0)

    def drain(ct, carry):
        own_o(ct).wait()

        def take_o(d, c):
            p = (me + d) % 8
            rc(ob.at[yh, ct, my_rows], orecv.at[p, ct], o_send.at[0, 0], o_recv.at[p, ct], member(p)).wait_recv()
            return c

        lax.fori_loop(1, 8, take_o, 0)
        return carry

    lax.fori_loop(0, COLS, drain, 0)

    for h in range(HEADS):
        parts = [orecv[h, ct].astype(jnp.float32) for ct in range(COLS)]
        for f in range(2):
            for r in range(2):
                n = (2 * f + r) * 24
                row = jnp.concatenate([p_[n : n + 24] for p_ in parts], axis=0)
                outv[f, r, :, h * DIM : (h + 1) * DIM] = row.astype(jnp.bfloat16)
    done = pltpu.make_async_copy(outv, out_hbm, out_sem)
    done.start()

    def sent(d, carry):
        p = (me + d) % 8
        for ct in range(COLS):
            kv_piece(ct, d).wait_send()
        q_piece(d).wait_send()
        return carry

    lax.fori_loop(1, 8, sent, 0)
    for c in started:
        c.wait_send()

    def sent_o(i, carry):
        for s in range(4):
            @pl.when((i % 2) * 4 + s != me)
            def _():
                o_piece(i, s).wait_send()
        return carry

    lax.fori_loop(0, 8, sent_o, 0)
    done.wait()


def solution(mesh):
    n_tm, n_rows = mesh.shape["tm"], mesh.shape["rows"]
    bf = jnp.bfloat16
    vm = pltpu.VMEM
    dma = pltpu.SemaphoreType.DMA

    def body(queries, keys, values, window_lists):
        any_ = pl.BlockSpec(memory_space=pl.ANY)
        return pl.pallas_call(
            functools.partial(kernel, n_tm, n_rows),
            out_shape=jax.ShapeDtypeStruct(queries.shape, bf),
            in_specs=[any_, any_, any_, pl.BlockSpec(memory_space=pltpu.SMEM)],
            out_specs=any_,
            scratch_shapes=[
                vm(queries.shape, bf), vm(queries.shape, bf), vm(queries.shape, bf),
                vm((HEADS, COLS, 2, PART, DIM), bf),
                vm((HEADS, COLS, PART, DIM), bf),
                vm((COLS, 4, 3, 2, TOK, DIM), bf),
                vm((2, COLS, TOK, DIM), bf),
                vm((WIN // 2, TOK, 2 * TOK), jnp.float32),
                vm((TOK, DIM), jnp.float32),
                vm((2, COLS, TOK, DIM), bf),
                vm((HEADS, COLS, PART, DIM), bf),
                vm(queries.shape, bf),
                dma((3,)), dma, dma((COLS, 8)), dma((COLS, 8)), dma((8,)), dma((8,)),
                dma((COLS, 2, 4)), dma((COLS, 2, 4)), dma((COLS, 2, 3)), dma((COLS, 2, 3)),
                dma((8, 4)), dma((8, COLS)), dma((2 * COLS + 1,)),
            ],
            compiler_params=pltpu.CompilerParams(
                collective_id=0, has_side_effects=True, vmem_limit_bytes=56 * 1024 * 1024
            ),
        )(queries, keys, values, window_lists.reshape(-1))

    row = P("tm", "rows", None, None)
    return jax.shard_map(body, mesh=mesh, in_specs=(row, row, row, P()), out_specs=row, check_vma=False)
```

```python
import functools

import jax
import jax.numpy as jnp
from jax import lax
from jax.experimental import pallas as pl
from jax.experimental.pallas import tpu as pltpu
from jax.sharding import PartitionSpec as P

HEADS = 8
COLS = 4
WIN = 12
TOK = 384
PART = 96
DIM = 128
LOG2E = 1.4426950408889634


def rc(src, dst, ss, rs, dev):
    return pltpu.make_async_remote_copy(
        src_ref=src, dst_ref=dst, send_sem=ss, recv_sem=rs, device_id=dev, device_id_type=pl.DeviceIdType.MESH
    )


def kernel(
    n_tm, n_rows, q_hbm, k_hbm, v_hbm, lists_hbm, out_hbm,
    lists, qin, kin, vin, skv, sq, kv01, kv2, kv3, qb, scores, peak, ob, orecv, outv,
    in_sem, out_sem, kv_send, kv_recv, q_send, q_recv, z_send, z_recv, x_send, x_recv,
    cx_send, cx_recv, cz_send, cz_recv, o_send, o_recv, loc_sem,
):
    tm = lax.axis_index("tm")
    rows = lax.axis_index("rows")
    x, yh = tm // 2, tm % 2
    z, part = rows // 4, rows % 4
    me = yh * 4 + part

    def member(p):
        return (x * 2 + p // 4, z * 4 + p % 4)

    z_up = (tm, (rows + 4) % n_rows)
    z_dn = (tm, (rows + n_rows - 4) % n_rows)
    x_up = ((tm + 2) % n_tm, rows)
    x_dn = ((tm + n_tm - 2) % n_tm, rows)

    loads = [
        pltpu.make_async_copy(src, dst, in_sem.at[i])
        for i, (src, dst) in enumerate(((k_hbm, kin), (v_hbm, vin), (q_hbm, qin), (lists_hbm, lists)))
    ]
    for c in loads:
        c.start()

    barrier = pltpu.get_barrier_semaphore()

    def greet(d, carry):
        pl.semaphore_signal(barrier, inc=1, device_id=member((me + d) % 8), device_id_type=pl.DeviceIdType.MESH)
        return carry

    lax.fori_loop(1, 8, greet, 0)
    for dev in (z_up, z_dn, x_up, x_dn):
        pl.semaphore_signal(barrier, inc=1, device_id=dev, device_id_type=pl.DeviceIdType.MESH)
    pl.semaphore_wait(barrier, 11)

    def pack(src, ct, p):
        feats = pl.ds(pl.multiple_of(p * DIM, DIM), DIM)
        pieces = []
        for f in range(2):
            for r in range(2):
                full = src[f, r, :, feats].astype(jnp.float32)
                pieces.append(full[ct * 24 : ct * 24 + 24])
        return jnp.concatenate(pieces, axis=0).astype(jnp.bfloat16)

    def rows_of(p):
        return pl.ds(pl.multiple_of((p % 4) * PART, PART), PART)

    my_rows = rows_of(me)

    def tile(ct, layer, row):
        return kv01.at[ct, layer, row] if ct < 2 else (kv2, kv3)[ct - 2].at[layer, row]

    def kv_piece(ct, p, source):
        return rc(
            skv.at[p, ct], tile(ct, 1 + source // 4, 1).at[:, rows_of(source)],
            kv_send.at[ct, p], kv_recv.at[ct, source], member(p),
        )

    def q_piece(p, source):
        return rc(
            sq.at[p], qb.at[source // 4, :, rows_of(source)], q_send.at[p], q_recv.at[source], member(p)
        )

    def z_piece(ct, up, p, packed=False):
        return rc(
            skv.at[p, ct] if packed else tile(ct, 1 + p // 4, 1).at[:, rows_of(p)],
            tile(ct, 1 + p // 4, 0 if up else 2).at[:, rows_of(p)],
            z_send.at[ct, up, p], z_recv.at[ct, up, p], z_up if up else z_dn,
        )

    def x_piece(ct, p, packed=False):
        late = p // 4
        dev = ((tm + 2 * late + n_tm - 2 * (1 - late)) % n_tm, rows)
        return rc(
            skv.at[p, ct] if packed else tile(ct, 1 + late, 1).at[:, rows_of(p)],
            tile(ct, 3 - 3 * late, 1).at[:, rows_of(p)],
            x_send.at[ct, p], x_recv.at[ct, p], dev,
        )

    def x_corner(ct, up, row):
        return rc(
            tile(ct, 2 if up else 1, row), tile(ct, 0 if up else 3, row),
            cx_send.at[ct, up, row // 2], cx_recv.at[ct, up, row // 2], x_up if up else x_dn,
        )

    def z_corner(ct, up):
        layer = 3 if up else 0
        return rc(
            tile(ct, layer, 1), tile(ct, layer, 0 if up else 2),
            cz_send.at[ct - 2, up], cz_recv.at[ct - 2, up], z_up if up else z_dn,
        )

    def x_corners(ct):
        return [x_corner(ct, up, row) for up, row in (((1, 0), (0, 2), (1, 2), (0, 0)) if ct < 2 else ((1, 0), (0, 2)))]

    def z_corners(ct):
        return [z_corner(ct, up) for up in (1, 0)]

    def own_copy(ct):
        return pltpu.make_async_copy(skv.at[me, ct], tile(ct, 1 + yh, 1).at[:, my_rows], loc_sem.at[ct])

    def each(first, f):
        def step(d, carry):
            f((me + d) % 2 + 2 * ((me // 2 + d // 2) % 2) + 4 * ((me // 4 + d // 4) % 2), d)
            return carry

        lax.fori_loop(first, 8, step, 0)

    def own_first(ct):
        skv[me, ct, 0] = pack(kin, ct, me)
        skv[me, ct, 1] = pack(vin, ct, me)
        own_copy(ct).start()
        for c in (z_piece(ct, 1, me, True), z_piece(ct, 0, me, True), x_piece(ct, me, True)):
            c.start()

    def send_kv(ct):
        def one(p, d):
            skv[p, ct, 0] = pack(kin, ct, p)
            skv[p, ct, 1] = pack(vin, ct, p)
            kv_piece(ct, p, me).start()

        each(1, one)

    def forward_z(ct):
        own_copy(ct).wait()

        def one(p, d):
            kv_piece(ct, p, p).wait_recv()
            z_piece(ct, 1, p).start()
            z_piece(ct, 0, p).start()
            if ct < 2:
                x_piece(ct, p).start()

        each(1, one)

    def forward_x(ct):
        each(1, lambda p, d: x_piece(ct, p).start())

    def arrived_z(ct):
        def one(p, d):
            z_piece(ct, 1, p).wait_recv()
            z_piece(ct, 0, p).wait_recv()

        each(0, one)

    def arrived_x(ct):
        each(0, lambda p, d: x_piece(ct, p).wait_recv())

    def begin(copies):
        for c in copies:
            c.start()

    def arrived(copies):
        for c in copies:
            c.wait_recv()

    scale = DIM ** -0.5 * LOG2E

    def o_piece(layer, ct, s):
        p = layer * 4 + s
        return rc(
            ob.at[layer, ct, pl.ds(s * PART, PART)], orecv.at[me, ct], o_send.at[ct, layer, s], o_recv.at[me, ct], member(p)
        )

    def own_o(ct):
        return pltpu.make_async_copy(ob.at[yh, ct, my_rows], orecv.at[me, ct], loc_sem.at[COLS + 1 + ct])

    def attend(layer, ct, reach):
        tile = ((2 * x + layer) * 8 + z) * COLS + ct

        def place(slot):
            listed = lists[slot, tile]
            present = listed >= 0
            t = jnp.where(present, listed, tile)
            t_layer, t_row, t_col = t // 32, (t // 4) % 8, t % 4
            return t_col, jnp.clip(t_layer - 2 * x + 1, 0, 3), jnp.clip(t_row - z + 1, 0, 2), jnp.where(present, 1.0, 0.0)

        def pick(c_, l_, r_, which):
            found = kv01[jnp.clip(c_, 0, 1), l_, r_, which]
            if reach > 1:
                found = jnp.where(c_ == 2, kv2[l_, r_, which], found)
            if reach > 2:
                found = jnp.where(c_ == 3, kv3[l_, r_, which], found)
            return found

        @pl.when(tm >= 0)
        def _():
            q = qb[layer, ct]
            high = jnp.full((TOK, DIM), -jnp.inf, jnp.float32)
            for j in range(WIN // 2):
                keys = []
                for slot in (2 * j, 2 * j + 1):
                    c_, l_, r_, _ = place(slot)
                    keys.append(pick(c_, l_, r_, 0))
                s = lax.dot_general(
                    q, jnp.concatenate(keys, axis=0), (((1,), (1,)), ((), ())), preferred_element_type=jnp.float32
                )
                scores[j] = s
                for b in range(2 * TOK // DIM):
                    high = jnp.maximum(high, s[:, b * DIM : (b + 1) * DIM])
            peak[...] = jnp.broadcast_to(jnp.max(high, axis=1, keepdims=True) * scale, (TOK, DIM))

        @pl.when(rows >= 0)
        def _():
            top = jnp.concatenate([peak[...]] * (2 * TOK // DIM), axis=1)
            acc = jnp.zeros((TOK, 2 * DIM), jnp.float32)
            for j in range(WIN // 2):
                vals = []
                for slot in (2 * j, 2 * j + 1):
                    c_, l_, r_, flag = place(slot)
                    flag = jnp.full((TOK, DIM), flag, jnp.float32).astype(jnp.bfloat16)
                    vals.append(jnp.concatenate((pick(c_, l_, r_, 1) * flag, flag), axis=1))
                w = jnp.exp2(scores[j] * scale - top).astype(jnp.bfloat16)
                acc = acc + jnp.dot(w, jnp.concatenate(vals, axis=0), preferred_element_type=jnp.float32)
            ob[layer, ct] = (acc[:, :DIM] / acc[:, DIM:]).astype(jnp.bfloat16)

    def finish(first, count, reach):
        def step(i, carry):
            layer, ct = i % 2, first + i // 2
            attend(layer, ct, reach)
            for s in range(4):
                @pl.when(layer * 4 + s != me)
                def _():
                    o_piece(layer, ct, s).start()

            @pl.when(layer == yh)
            def _():
                own_o(ct).start()

            return carry

        lax.fori_loop(0, 2 * count, step, 0)

    def own_q():
        return pltpu.make_async_copy(sq.at[me], qb.at[yh, :, my_rows], loc_sem.at[COLS])

    def send_q():
        def one(p, d):
            for ct in range(COLS):
                sq[p, ct] = pack(qin, ct, p)

            @pl.when(d > 0)
            def _():
                q_piece(p, me).start()

        each(0, one)
        own_q().start()

    loads[0].wait()
    loads[1].wait()
    own_first(0)
    send_kv(0)
    own_first(1)
    own_first(2)
    own_first(3)
    send_kv(1)
    forward_z(0)
    send_kv(2)
    forward_z(1)
    send_kv(3)
    loads[2].wait()
    send_q()
    arrived_z(0)
    begin(x_corners(0))
    forward_z(2)
    arrived_z(1)
    begin(x_corners(1))
    forward_x(2)
    forward_z(3)
    forward_x(3)
    arrived_z(2)
    begin(x_corners(2))
    own_q().wait()
    loads[3].wait()
    each(1, lambda p, d: q_piece(p, p).wait_recv())
    for ct in (0, 1):
        arrived_x(ct)
        arrived(x_corners(ct))
    arrived_x(2)
    begin(z_corners(2))
    finish(0, 1, 1)
    arrived_z(3)
    begin(x_corners(3))
    arrived_x(3)
    begin(z_corners(3))
    arrived(x_corners(2))
    arrived(z_corners(2))
    finish(1, 1, 2)
    arrived(x_corners(3))
    arrived(z_corners(3))
    finish(2, 2, 3)

    def drain(ct, carry):
        own_o(ct).wait()

        def take_o(p, d):
            rc(
                ob.at[yh, ct, my_rows], orecv.at[p, ct], o_send.at[ct, 0, 0], o_recv.at[p, ct], member(p)
            ).wait_recv()

        each(1, take_o)
        return carry

    lax.fori_loop(0, COLS, drain, 0)

    for h in range(HEADS):
        parts = [orecv[h, ct].astype(jnp.float32) for ct in range(COLS)]
        for f in range(2):
            for r in range(2):
                n = (2 * f + r) * 24
                row = jnp.concatenate([p_[n : n + 24] for p_ in parts], axis=0)
                outv[f, r, :, h * DIM : (h + 1) * DIM] = row.astype(jnp.bfloat16)
    done = pltpu.make_async_copy(outv, out_hbm, out_sem)
    done.start()

    def sent(p, d):
        for ct in range(COLS):
            @pl.when(d > 0)
            def _():
                kv_piece(ct, p, me).wait_send()

            z_piece(ct, 1, p).wait_send()
            z_piece(ct, 0, p).wait_send()
            x_piece(ct, p).wait_send()

        @pl.when(d > 0)
        def _():
            q_piece(p, me).wait_send()

    each(0, sent)
    for ct in range(COLS):
        for c in x_corners(ct) + (z_corners(ct) if ct > 1 else []):
            c.wait_send()

    def sent_o(i, carry):
        for s in range(4):
            @pl.when((i % 2) * 4 + s != me)
            def _():
                o_piece(i % 2, i // 2, s).wait_send()
        return carry

    lax.fori_loop(0, 8, sent_o, 0)
    done.wait()


def solution(mesh):
    n_tm, n_rows = mesh.shape["tm"], mesh.shape["rows"]
    bf = jnp.bfloat16
    vm = pltpu.VMEM
    dma = pltpu.SemaphoreType.DMA

    def body(queries, keys, values, window_lists):
        any_ = pl.BlockSpec(memory_space=pl.ANY)
        return pl.pallas_call(
            functools.partial(kernel, n_tm, n_rows),
            out_shape=jax.ShapeDtypeStruct(queries.shape, bf),
            in_specs=[any_, any_, any_, any_],
            out_specs=any_,
            scratch_shapes=[
                pltpu.SMEM(window_lists.shape[::-1], jnp.int32),
                vm(queries.shape, bf), vm(queries.shape, bf), vm(queries.shape, bf),
                vm((HEADS, COLS, 2, PART, DIM), bf),
                vm((HEADS, COLS, PART, DIM), bf),
                vm((2, 4, 3, 2, TOK, DIM), bf), vm((4, 3, 2, TOK, DIM), bf), vm((4, 3, 2, TOK, DIM), bf),
                vm((2, COLS, TOK, DIM), bf),
                vm((WIN // 2, TOK, 2 * TOK), jnp.float32),
                vm((TOK, DIM), jnp.float32),
                vm((2, COLS, TOK, DIM), bf),
                vm((HEADS, COLS, PART, DIM), bf),
                vm(queries.shape, bf),
                dma((4,)), dma, dma((COLS, 8)), dma((COLS, 8)), dma((8,)), dma((8,)),
                dma((COLS, 2, 8)), dma((COLS, 2, 8)), dma((COLS, 8)), dma((COLS, 8)),
                dma((COLS, 2, 2)), dma((COLS, 2, 2)), dma((2, 2)), dma((2, 2)),
                dma((COLS, 2, 4)), dma((8, COLS)), dma((2 * COLS + 1,)),
            ],
            compiler_params=pltpu.CompilerParams(
                collective_id=0, has_side_effects=True, vmem_limit_bytes=56 * 1024 * 1024
            ),
        )(queries, keys, values, window_lists.T)

    row = P("tm", "rows", None, None)
    return jax.shard_map(body, mesh=mesh, in_specs=(row, row, row, P()), out_specs=row, check_vma=False)
```

```python
import functools

import jax
import jax.numpy as jnp
from jax import lax
from jax.experimental import pallas as pl
from jax.experimental.pallas import tpu as pltpu
from jax.sharding import PartitionSpec as P

HEADS = 8
COLS = 4
WIN = 12
TOK = 384
PART = 96
DIM = 128
LOG2E = 1.4426950408889634


def rc(src, dst, ss, rs, dev):
    return pltpu.make_async_remote_copy(
        src_ref=src, dst_ref=dst, send_sem=ss, recv_sem=rs, device_id=dev, device_id_type=pl.DeviceIdType.MESH
    )


def kernel(
    n_tm, n_rows, q_hbm, k_hbm, v_hbm, lists_hbm, out_hbm,
    lists, qin, kin, vin, skv, sq, kv01, kv2, kv3, qb, scores, peak, ob, orecv, outv,
    in_sem, out_sem, kv_send, kv_recv, q_send, q_recv, z_send, z_recv, x_send, x_recv,
    cx_send, cx_recv, cz_send, cz_recv, o_send, o_recv, loc_sem,
):
    tm = lax.axis_index("tm")
    rows = lax.axis_index("rows")
    x, yh = tm // 2, tm % 2
    z, part = rows // 4, rows % 4
    me = yh * 4 + part

    def member(p):
        return (x * 2 + p // 4, z * 4 + p % 4)

    z_up = (tm, (rows + 4) % n_rows)
    z_dn = (tm, (rows + n_rows - 4) % n_rows)
    x_up = ((tm + 2) % n_tm, rows)
    x_dn = ((tm + n_tm - 2) % n_tm, rows)

    loads = [
        pltpu.make_async_copy(src, dst, in_sem.at[i])
        for i, (src, dst) in enumerate(((k_hbm, kin), (v_hbm, vin), (q_hbm, qin), (lists_hbm, lists)))
    ]
    for c in loads:
        c.start()

    barrier = pltpu.get_barrier_semaphore()

    def greet(d, carry):
        pl.semaphore_signal(barrier, inc=1, device_id=member((me + d) % 8), device_id_type=pl.DeviceIdType.MESH)
        return carry

    lax.fori_loop(1, 8, greet, 0)
    for dev in (z_up, z_dn, x_up, x_dn):
        pl.semaphore_signal(barrier, inc=1, device_id=dev, device_id_type=pl.DeviceIdType.MESH)
    pl.semaphore_wait(barrier, 11)

    def pack(src, ct, p):
        feats = pl.ds(pl.multiple_of(p * DIM, DIM), DIM)
        pieces = []
        for f in range(2):
            for r in range(2):
                full = src[f, r, :, feats].astype(jnp.float32)
                pieces.append(full[ct * 24 : ct * 24 + 24])
        return jnp.concatenate(pieces, axis=0).astype(jnp.bfloat16)

    def rows_of(p):
        return pl.ds(pl.multiple_of((p % 4) * PART, PART), PART)

    my_rows = rows_of(me)

    def tile(ct, layer, row):
        return kv01.at[ct, layer, row] if ct < 2 else (kv2, kv3)[ct - 2].at[layer, row]

    def kv_piece(ct, p, source):
        return rc(
            skv.at[p, ct], tile(ct, 1 + source // 4, 1).at[:, rows_of(source)],
            kv_send, kv_recv.at[ct, source], member(p),
        )

    def q_piece(p, source):
        return rc(
            sq.at[p], qb.at[source // 4, :, rows_of(source)], q_send, q_recv, member(p)
        )

    def z_piece(ct, up, p, packed=False):
        return rc(
            skv.at[p, ct] if packed else tile(ct, 1 + p // 4, 1).at[:, rows_of(p)],
            tile(ct, 1 + p // 4, 0 if up else 2).at[:, rows_of(p)],
            z_send, z_recv.at[ct, up], z_up if up else z_dn,
        )

    def x_piece(ct, p, packed=False):
        late = p // 4
        dev = ((tm + 2 * late + n_tm - 2 * (1 - late)) % n_tm, rows)
        return rc(
            skv.at[p, ct] if packed else tile(ct, 1 + late, 1).at[:, rows_of(p)],
            tile(ct, 3 - 3 * late, 1).at[:, rows_of(p)],
            x_send, x_recv.at[ct, late], dev,
        )

    def x_corner(ct, up, row):
        return rc(
            tile(ct, 2 if up else 1, row), tile(ct, 0 if up else 3, row),
            cx_send, cx_recv.at[ct, up], x_up if up else x_dn,
        )

    def z_corner(ct, up):
        layer = 3 if up else 0
        return rc(
            tile(ct, layer, 1), tile(ct, layer, 0 if up else 2),
            cz_send, cz_recv.at[ct - 2, up], z_up if up else z_dn,
        )

    def x_corners(ct):
        return [x_corner(ct, up, row) for up, row in (((1, 0), (0, 2), (1, 2), (0, 0)) if ct < 2 else ((1, 0), (0, 2)))]

    def z_corners(ct):
        return [z_corner(ct, up) for up in (1, 0)]

    def own_copy(ct):
        return pltpu.make_async_copy(skv.at[me, ct], tile(ct, 1 + yh, 1).at[:, my_rows], loc_sem.at[ct])

    def each(first, f):
        def step(d, carry):
            f((me + d) % 8, d)
            return carry

        lax.fori_loop(first, 8, step, 0)

    def own_first(ct):
        skv[me, ct, 0] = pack(kin, ct, me)
        skv[me, ct, 1] = pack(vin, ct, me)
        own_copy(ct).start()
        for c in (z_piece(ct, 1, me, True), z_piece(ct, 0, me, True), x_piece(ct, me, True)):
            c.start()

    def send_kv(ct):
        def one(p):
            skv[p, ct, 0] = pack(kin, ct, p)
            skv[p, ct, 1] = pack(vin, ct, p)
            kv_piece(ct, p, me).start()

        return one

    def forward_z(ct, x_too, following=None):
        own_copy(ct).wait()

        def one(partner, d):
            p = (me + 8 - d) % 8
            kv_piece(ct, p, p).wait_recv()
            z_piece(ct, 1, p).start()
            z_piece(ct, 0, p).start()
            if x_too:
                x_piece(ct, p).start()
            if following is not None:
                following(partner)

        each(1, one)

    def forward_x(ct):
        each(1, lambda p, d: x_piece(ct, p).start())

    def landed(ref, sem):
        rc(ref, ref, kv_send, sem, z_up).wait_recv()

    def gone(ref, sem):
        rc(ref, ref, sem, q_recv, z_up).wait_send()

    def block(ct):
        return kv01.at[ct] if ct < 2 else (kv2, kv3)[ct - 2]

    def arrived_z(ct):
        for up in (1, 0):
            landed(block(ct).at[1:3, 0 if up else 2], z_recv.at[ct, up])

    def arrived_x(ct):
        for late in (1, 0):
            landed(tile(ct, 3 - 3 * late, 1), x_recv.at[ct, late])

    def arrived_x_corners(ct):
        for up in (1, 0):
            landed(block(ct).at[0 if up else 3, 0 : (2 if ct < 2 else 1)], cx_recv.at[ct, up])

    def begin(copies):
        for c in copies:
            c.start()

    def arrived(copies):
        for c in copies:
            c.wait_recv()

    scale = DIM ** -0.5 * LOG2E

    def o_piece(layer, ct, s):
        p = layer * 4 + s
        return rc(
            ob.at[layer, ct, pl.ds(s * PART, PART)], orecv.at[me, ct], o_send, o_recv.at[ct], member(p)
        )

    def own_o(ct):
        return pltpu.make_async_copy(ob.at[yh, ct, my_rows], orecv.at[me, ct], loc_sem.at[COLS + 1])

    def attend(layer, ct, reach):
        tile = ((2 * x + layer) * 8 + z) * COLS + ct

        def place(slot):
            listed = lists[slot, tile]
            present = listed >= 0
            t = jnp.where(present, listed, tile)
            t_layer, t_row, t_col = t // 32, (t // 4) % 8, t % 4
            return t_col, jnp.clip(t_layer - 2 * x + 1, 0, 3), jnp.clip(t_row - z + 1, 0, 2), jnp.where(present, 1.0, 0.0)

        def pick(c_, l_, r_, which):
            found = kv01[jnp.clip(c_, 0, 1), l_, r_, which]
            if reach > 1:
                found = jnp.where(c_ == 2, kv2[l_, r_, which], found)
            if reach > 2:
                found = jnp.where(c_ == 3, kv3[l_, r_, which], found)
            return found

        @pl.when(tm >= 0)
        def _():
            q = qb[layer, ct]
            high = jnp.full((TOK, DIM), -jnp.inf, jnp.float32)
            for j in range(WIN // 2):
                keys = []
                for slot in (2 * j, 2 * j + 1):
                    c_, l_, r_, _ = place(slot)
                    keys.append(pick(c_, l_, r_, 0))
                s = lax.dot_general(
                    q, jnp.concatenate(keys, axis=0), (((1,), (1,)), ((), ())), preferred_element_type=jnp.float32
                )
                scores[j] = s
                for b in range(2 * TOK // DIM):
                    high = jnp.maximum(high, s[:, b * DIM : (b + 1) * DIM])
            peak[...] = jnp.broadcast_to(jnp.max(high, axis=1, keepdims=True) * scale, (TOK, DIM))

        @pl.when(rows >= 0)
        def _():
            top = jnp.concatenate([peak[...]] * (2 * TOK // DIM), axis=1)
            acc = jnp.zeros((TOK, 2 * DIM), jnp.float32)
            for j in range(WIN // 2):
                vals = []
                for slot in (2 * j, 2 * j + 1):
                    c_, l_, r_, flag = place(slot)
                    flag = jnp.full((TOK, DIM), flag, jnp.float32).astype(jnp.bfloat16)
                    vals.append(jnp.concatenate((pick(c_, l_, r_, 1) * flag, flag), axis=1))
                w = jnp.exp2(scores[j] * scale - top).astype(jnp.bfloat16)
                acc = acc + jnp.dot(w, jnp.concatenate(vals, axis=0), preferred_element_type=jnp.float32)
            ob[layer, ct] = (acc[:, :DIM] / acc[:, DIM:]).astype(jnp.bfloat16)

    def finish(first, count, reach):
        def step(i, carry):
            layer, ct = i % 2, first + i // 2
            attend(layer, ct, reach)
            for s in range(4):
                @pl.when(layer * 4 + s != me)
                def _():
                    o_piece(layer, ct, s).start()

            @pl.when(layer == yh)
            def _():
                own_o(ct).start()

            return carry

        lax.fori_loop(0, 2 * count, step, 0)

    def own_q():
        return pltpu.make_async_copy(sq.at[me], qb.at[yh, :, my_rows], loc_sem.at[COLS])

    def pack_q(p):
        for ct in range(COLS):
            sq[p, ct] = pack(qin, ct, p)

    def send_q(p):
        pack_q(p)
        q_piece(p, me).start()

    loads[0].wait()
    loads[1].wait()
    own_first(0)
    each(1, lambda p, d: send_kv(0)(p))
    own_first(1)
    forward_z(0, True, send_kv(1))
    own_first(2)
    forward_z(1, True, send_kv(2))
    arrived_z(0)
    begin(x_corners(0))
    own_first(3)
    forward_z(2, False, send_kv(3))
    forward_x(2)
    arrived_z(1)
    begin(x_corners(1))
    loads[2].wait()
    forward_z(3, True, send_q)
    pack_q(me)
    own_q().start()
    arrived_z(2)
    begin(x_corners(2))
    own_q().wait()
    loads[3].wait()
    landed(sq.at[0:7], q_recv)
    for ct in (0, 1):
        arrived_x(ct)
        arrived_x_corners(ct)
    arrived_x(2)
    begin(z_corners(2))
    finish(0, 1, 1)
    arrived_z(3)
    begin(x_corners(3))
    arrived_x(3)
    begin(z_corners(3))
    arrived_x_corners(2)
    arrived(z_corners(2))
    finish(1, 1, 2)
    arrived_x_corners(3)
    arrived(z_corners(3))
    finish(2, 2, 3)

    pltpu.make_async_copy(orecv.at[me], orecv.at[me], loc_sem.at[COLS + 1]).wait()
    for ct in range(COLS):
        landed(orecv.at[0:7, ct], o_recv.at[ct])

    for h in range(HEADS):
        parts = [orecv[h, ct].astype(jnp.float32) for ct in range(COLS)]
        for f in range(2):
            for r in range(2):
                n = (2 * f + r) * 24
                row = jnp.concatenate([p_[n : n + 24] for p_ in parts], axis=0)
                outv[f, r, :, h * DIM : (h + 1) * DIM] = row.astype(jnp.bfloat16)
    done = pltpu.make_async_copy(outv, out_hbm, out_sem)
    done.start()

    gone(skv.at[0:7], kv_send)
    gone(sq.at[0:7], q_send)
    gone(kv01.at[:, :, 0:2], z_send)
    gone(kv2.at[:, 0:2], x_send)
    gone(kv01.at[0], cx_send)
    gone(kv2.at[:, 0], cz_send)
    gone(orecv.at[0:7], o_send)
    done.wait()


def solution(mesh):
    n_tm, n_rows = mesh.shape["tm"], mesh.shape["rows"]
    bf = jnp.bfloat16
    vm = pltpu.VMEM
    dma = pltpu.SemaphoreType.DMA

    def body(queries, keys, values, window_lists):
        any_ = pl.BlockSpec(memory_space=pl.ANY)
        return pl.pallas_call(
            functools.partial(kernel, n_tm, n_rows),
            out_shape=jax.ShapeDtypeStruct(queries.shape, bf),
            in_specs=[any_, any_, any_, any_],
            out_specs=any_,
            scratch_shapes=[
                pltpu.SMEM(window_lists.shape[::-1], jnp.int32),
                vm(queries.shape, bf), vm(queries.shape, bf), vm(queries.shape, bf),
                vm((HEADS, COLS, 2, PART, DIM), bf),
                vm((HEADS, COLS, PART, DIM), bf),
                vm((2, 4, 3, 2, TOK, DIM), bf), vm((4, 3, 2, TOK, DIM), bf), vm((4, 3, 2, TOK, DIM), bf),
                vm((2, COLS, TOK, DIM), bf),
                vm((WIN // 2, TOK, 2 * TOK), jnp.float32),
                vm((TOK, DIM), jnp.float32),
                vm((2, COLS, TOK, DIM), bf),
                vm((HEADS, COLS, PART, DIM), bf),
                vm(queries.shape, bf),
                dma((4,)), dma, dma, dma((COLS, 8)), dma, dma, dma, dma((COLS, 2)), dma, dma((COLS, 2)),
                dma, dma((COLS, 2)), dma, dma((2, 2)), dma, dma((COLS,)), dma((COLS + 2,)),
            ],
            compiler_params=pltpu.CompilerParams(
                collective_id=0, has_side_effects=True, vmem_limit_bytes=56 * 1024 * 1024
            ),
        )(queries, keys, values, window_lists.T)

    row = P("tm", "rows", None, None)
    return jax.shard_map(body, mesh=mesh, in_specs=(row, row, row, P()), out_specs=row, check_vma=False)
```

```python
import functools

import jax
import jax.numpy as jnp
from jax import lax
from jax.experimental import pallas as pl
from jax.experimental.pallas import tpu as pltpu
from jax.sharding import PartitionSpec as P

HEADS = 8
COLS = 4
WIN = 12
TOK = 384
PART = 96
DIM = 128
LOG2E = 1.4426950408889634


def rc(src, dst, ss, rs, dev):
    return pltpu.make_async_remote_copy(
        src_ref=src, dst_ref=dst, send_sem=ss, recv_sem=rs, device_id=dev, device_id_type=pl.DeviceIdType.MESH
    )


def kernel(
    n_tm, n_rows, q_hbm, k_hbm, v_hbm, lists_hbm, out_ref,
    lists, qin, kin, vin, skv, sq, kv01, kv2, kv3, far2, qb, scores, peak, held, held_peak, ob, orecv,
    in_sem, kv_send, kv_recv, q_send, q_recv, z_send, z_recv, x_send, x_recv,
    cx_send, cx_recv, cz_send, cz_recv, o_send, o_recv, loc_sem,
):
    tm = lax.axis_index("tm")
    rows = lax.axis_index("rows")
    x, yh = tm // 2, tm % 2
    z, part = rows // 4, rows % 4
    me = yh * 4 + part

    def member(p):
        return (x * 2 + p // 4, z * 4 + p % 4)

    z_up = (tm, (rows + 4) % n_rows)
    z_dn = (tm, (rows + n_rows - 4) % n_rows)
    x_up = ((tm + 2) % n_tm, rows)
    x_dn = ((tm + n_tm - 2) % n_tm, rows)

    loads = [
        pltpu.make_async_copy(src, dst, in_sem.at[i])
        for i, (src, dst) in enumerate(((k_hbm, kin), (v_hbm, vin), (q_hbm, qin), (lists_hbm, lists)))
    ]
    for c in loads:
        c.start()

    barrier = pltpu.get_barrier_semaphore()

    def greet(d, carry):
        pl.semaphore_signal(barrier, inc=1, device_id=member((me + d) % 8), device_id_type=pl.DeviceIdType.MESH)
        return carry

    lax.fori_loop(1, 8, greet, 0)
    for dev in (z_up, z_dn, x_up, x_dn):
        pl.semaphore_signal(barrier, inc=1, device_id=dev, device_id_type=pl.DeviceIdType.MESH)
    pl.semaphore_wait(barrier, 11)

    def pack(src, ct, p):
        feats = pl.ds(pl.multiple_of(p * DIM, DIM), DIM)
        pieces = []
        for f in range(2):
            for r in range(2):
                full = src[f, r, :, feats].astype(jnp.float32)
                pieces.append(full[ct * 24 : ct * 24 + 24])
        return jnp.concatenate(pieces, axis=0).astype(jnp.bfloat16)

    def rows_of(p):
        return pl.ds(pl.multiple_of((p % 4) * PART, PART), PART)

    my_rows = rows_of(me)

    def tile(ct, layer, row):
        if ct == 2 and not hasattr(layer, "dtype") and layer in (0, 3) and row != 1:
            return far2.at[layer // 3, row // 2]
        return kv01.at[ct, layer, row] if ct < 2 else (kv2, kv3)[ct - 2].at[layer, row]

    def kv_piece(ct, p, source):
        return rc(
            skv.at[p, ct], tile(ct, 1 + source // 4, 1).at[:, rows_of(source)],
            kv_send, kv_recv.at[ct, source], member(p),
        )

    def q_piece(p, source):
        return rc(
            sq.at[p], qb.at[source // 4, :, rows_of(source)], q_send, q_recv, member(p)
        )

    def z_piece(ct, up, p, packed=False):
        return rc(
            skv.at[p, ct] if packed else tile(ct, 1 + p // 4, 1).at[:, rows_of(p)],
            tile(ct, 1 + p // 4, 0 if up else 2).at[:, rows_of(p)],
            z_send, z_recv.at[ct, up], z_up if up else z_dn,
        )

    def x_piece(ct, p, packed=False):
        late = p // 4
        dev = ((tm + 2 * late + n_tm - 2 * (1 - late)) % n_tm, rows)
        return rc(
            skv.at[p, ct] if packed else tile(ct, 1 + late, 1).at[:, rows_of(p)],
            tile(ct, 3 - 3 * late, 1).at[:, rows_of(p)],
            x_send, x_recv.at[ct, late], dev,
        )

    def x_corner(ct, up, row):
        return rc(
            tile(ct, 2 if up else 1, row), tile(ct, 0 if up else 3, row),
            cx_send, cx_recv.at[ct, up], x_up if up else x_dn,
        )

    def z_corner(ct, up):
        layer = 3 if up else 0
        return rc(
            tile(ct, layer, 1), tile(ct, layer, 0 if up else 2),
            cz_send, cz_recv.at[ct - 2, up], z_up if up else z_dn,
        )

    def x_corners(ct):
        return [x_corner(ct, up, row) for up, row in (((1, 0), (0, 2), (1, 2), (0, 0)) if ct < 2 else ((1, 0), (0, 2)))]

    def z_corners(ct):
        return [z_corner(ct, up) for up in (1, 0)]

    def own_copy(ct):
        return pltpu.make_async_copy(skv.at[me, ct], tile(ct, 1 + yh, 1).at[:, my_rows], loc_sem.at[ct])

    def each(first, f):
        def step(d, carry):
            d = d // 2 + 4 * (d % 2)
            f((me + d) % 8, d)
            return carry

        lax.fori_loop(first, 8, step, 0)

    def own_first(ct):
        skv[me, ct, 0] = pack(kin, ct, me)
        skv[me, ct, 1] = pack(vin, ct, me)
        own_copy(ct).start()
        for c in (z_piece(ct, 1, me, True), z_piece(ct, 0, me, True), x_piece(ct, me, True)):
            c.start()

    def send_kv(ct):
        def one(p):
            skv[p, ct, 0] = pack(kin, ct, p)
            skv[p, ct, 1] = pack(vin, ct, p)
            kv_piece(ct, p, me).start()

        return one

    def forward_z(ct, x_too, following=None):
        own_copy(ct).wait()

        def one(partner, d):
            p = (me + 8 - d) % 8
            kv_piece(ct, p, p).wait_recv()
            z_piece(ct, 1, p).start()
            z_piece(ct, 0, p).start()
            if x_too:
                x_piece(ct, p).start()
            if following is not None:
                following(partner)

        each(1, one)

    def forward_x(ct):
        each(1, lambda p, d: x_piece(ct, p).start())

    def landed(ref, sem):
        rc(ref, ref, kv_send, sem, z_up).wait_recv()

    def gone(ref, sem):
        rc(ref, ref, sem, q_recv, z_up).wait_send()

    def block(ct):
        return kv01.at[ct] if ct < 2 else (kv2, kv3)[ct - 2]

    def arrived_z(ct):
        for up in (1, 0):
            landed(block(ct).at[1:3, 0 if up else 2], z_recv.at[ct, up])

    def arrived_x(ct):
        for late in (1, 0):
            landed(tile(ct, 3 - 3 * late, 1), x_recv.at[ct, late])

    def arrived_x_corners(ct):
        for up in (1, 0):
            landed(kv01.at[0, 0 if up else 3, 0 : (2 if ct < 2 else 1)], cx_recv.at[ct, up])

    def begin(copies):
        for c in copies:
            c.start()

    def arrived(copies):
        for c in copies:
            c.wait_recv()

    scale = DIM ** -0.5 * LOG2E

    def o_piece(layer, ct, s):
        p = layer * 4 + s
        return rc(
            ob.at[layer, ct, pl.ds(s * PART, PART)], orecv.at[me, ct], o_send, o_recv.at[ct], member(p)
        )

    def own_o(ct):
        return pltpu.make_async_copy(ob.at[yh, ct, my_rows], orecv.at[me, ct], loc_sem.at[COLS + 1])

    def attend(layer, ct, reach):
        tile_id = ((2 * x + layer) * 8 + z) * COLS + ct

        def place(slot):
            listed = lists[slot, tile_id]
            present = listed >= 0
            if reach == 2:
                f_layer, f_row, f_col = listed // 32, (listed // 4) % 8, listed % 4
                present = present & ~far(f_col, f_layer - 2 * x + 1, f_row - z + 1)
            t = jnp.where(present, listed, tile_id)
            t_layer, t_row, t_col = t // 32, (t // 4) % 8, t % 4
            return t_col, jnp.clip(t_layer - 2 * x + 1, 0, 3), jnp.clip(t_row - z + 1, 0, 2), jnp.where(present, 1.0, 0.0)

        def pick(c_, l_, r_, which):
            found = kv01[jnp.clip(c_, 0, 1), l_, r_, which]
            if reach > 1:
                found = jnp.where(c_ == 2, kv2[l_, r_, which], found)
            if reach > 2:
                found = jnp.where(c_ == 3, kv3[l_, r_, which], found)
                found = jnp.where(far(c_, l_, r_), far2[l_ // 3, r_ // 2, which], found)
            return found

        def far(c_, l_, r_):
            return (c_ == 2) & ((l_ == 0) | (l_ == 3)) & (r_ != 1)

        @pl.when(tm >= 0)
        def _():
            q = qb[layer, ct]
            high = jnp.full((TOK, DIM), -jnp.inf, jnp.float32)
            for j in range(WIN // 2):
                keys = []
                for slot in (2 * j, 2 * j + 1):
                    c_, l_, r_, _ = place(slot)
                    keys.append(pick(c_, l_, r_, 0))
                s = lax.dot_general(
                    q, jnp.concatenate(keys, axis=0), (((1,), (1,)), ((), ())), preferred_element_type=jnp.float32
                )
                scores[j] = s
                for b in range(2 * TOK // DIM):
                    high = jnp.maximum(high, s[:, b * DIM : (b + 1) * DIM])
            peak[...] = jnp.broadcast_to(jnp.max(high, axis=1, keepdims=True) * scale, (TOK, DIM))

        @pl.when(rows >= 0)
        def _():
            top = jnp.concatenate([peak[...]] * (2 * TOK // DIM), axis=1)
            acc = jnp.zeros((TOK, 2 * DIM), jnp.float32)
            for j in range(WIN // 2):
                vals = []
                for slot in (2 * j, 2 * j + 1):
                    c_, l_, r_, flag = place(slot)
                    flag = jnp.full((TOK, DIM), flag, jnp.float32).astype(jnp.bfloat16)
                    vals.append(jnp.concatenate((pick(c_, l_, r_, 1) * flag, flag), axis=1))
                w = jnp.exp2(scores[j] * scale - top).astype(jnp.bfloat16)
                acc = acc + jnp.dot(w, jnp.concatenate(vals, axis=0), preferred_element_type=jnp.float32)
            if reach == 2:
                held[layer] = acc
                held_peak[layer] = peak[...]
            else:
                ob[layer, ct] = (acc[:, :DIM] / acc[:, DIM:]).astype(jnp.bfloat16)

    def attend_far(layer, ct):
        tile_id = ((2 * x + layer) * 8 + z) * COLS + ct
        there = []
        for row in (-1, 1):
            corner = ((2 * x - 1 + 3 * layer) * 8 + z + row) * COLS + 2
            hits = [jnp.where(lists[slot, tile_id] == corner, 1.0, 0.0) for slot in range(WIN)]
            there.append(functools.reduce(jnp.maximum, hits))

        @pl.when(tm >= 0)
        def _():
            keys = jnp.concatenate([far2[layer, row, 0] for row in (0, 1)], axis=0)
            s = lax.dot_general(
                qb[layer, ct], keys, (((1,), (1,)), ((), ())), preferred_element_type=jnp.float32
            )
            high = jnp.full((TOK, DIM), -1e30, jnp.float32)
            for row in range(2):
                part_s = s[:, row * TOK : (row + 1) * TOK] + (there[row] - 1.0) * 1e30
                scores[0, :, row * TOK : (row + 1) * TOK] = part_s
                for b in range(TOK // DIM):
                    high = jnp.maximum(high, part_s[:, b * DIM : (b + 1) * DIM])
            peak[...] = jnp.maximum(
                held_peak[layer], jnp.broadcast_to(jnp.max(high, axis=1, keepdims=True) * scale, (TOK, DIM))
            )

        @pl.when(rows >= 0)
        def _():
            top = jnp.concatenate([peak[...]] * (2 * TOK // DIM), axis=1)
            vals = []
            for row in range(2):
                flag = jnp.full((TOK, DIM), there[row], jnp.float32).astype(jnp.bfloat16)
                vals.append(jnp.concatenate((far2[layer, row, 1] * flag, flag), axis=1))
            w = jnp.exp2(scores[0] * scale - top).astype(jnp.bfloat16)
            keep = jnp.exp2(held_peak[layer] - peak[...])
            acc = held[layer] * jnp.concatenate((keep, keep), axis=1) + jnp.dot(
                w, jnp.concatenate(vals, axis=0), preferred_element_type=jnp.float32
            )
            ob[layer, ct] = (acc[:, :DIM] / acc[:, DIM:]).astype(jnp.bfloat16)

    def hold(layer, carry):
        attend(layer, 1, 2)
        return carry

    def finish(first, count, work):
        def step(i, carry):
            layer, ct = i % 2, first + i // 2
            work(layer, ct)
            for s in range(4):
                @pl.when(layer * 4 + s != me)
                def _():
                    o_piece(layer, ct, s).start()

            @pl.when(layer == yh)
            def _():
                own_o(ct).start()

            return carry

        lax.fori_loop(0, 2 * count, step, 0)

    def own_q():
        return pltpu.make_async_copy(sq.at[me], qb.at[yh, :, my_rows], loc_sem.at[COLS])

    def pack_q(p):
        for ct in range(COLS):
            sq[p, ct] = pack(qin, ct, p)

    def send_q(p):
        pack_q(p)
        q_piece(p, me).start()

    loads[0].wait()
    loads[1].wait()
    own_first(0)
    each(1, lambda p, d: send_kv(0)(p))
    own_first(1)
    forward_z(0, True, send_kv(1))
    own_first(2)
    forward_z(1, True, send_kv(2))
    arrived_z(0)
    begin(x_corners(0))
    own_first(3)
    forward_z(2, False, send_kv(3))
    arrived_z(1)
    begin(x_corners(1))
    forward_x(2)
    loads[2].wait()
    forward_z(3, True, send_q)
    pack_q(me)
    own_q().start()
    arrived_z(2)
    begin(x_corners(2))
    own_q().wait()
    loads[3].wait()
    landed(sq.at[0:7], q_recv)
    for ct in (0, 1):
        arrived_x(ct)
        arrived_x_corners(ct)
    finish(0, 1, lambda layer, ct: attend(layer, ct, 1))
    arrived_x(2)
    begin(z_corners(2))
    arrived_z(3)
    begin(x_corners(3))
    arrived_x(3)
    begin(z_corners(3))
    lax.fori_loop(0, 2, hold, 0)
    arrived_x_corners(2)
    arrived(z_corners(2))
    finish(1, 1, attend_far)
    arrived_x_corners(3)
    arrived(z_corners(3))
    finish(2, 2, lambda layer, ct: attend(layer, ct, 3))

    pltpu.make_async_copy(orecv.at[me], orecv.at[me], loc_sem.at[COLS + 1]).wait()
    for ct in range(COLS):
        landed(orecv.at[0:7, ct], o_recv.at[ct])

    for h in range(HEADS):
        parts = [orecv[h, ct].astype(jnp.float32) for ct in range(COLS)]
        for f in range(2):
            for r in range(2):
                n = (2 * f + r) * 24
                row = jnp.concatenate([p_[n : n + 24] for p_ in parts], axis=0)
                out_ref[f, r, :, h * DIM : (h + 1) * DIM] = row.astype(jnp.bfloat16)

    gone(skv.at[0:7], kv_send)
    gone(sq.at[0:7], q_send)
    gone(kv01.at[:, :, 0:2], z_send)
    gone(kv2.at[:, 0:2], x_send)
    gone(kv01.at[0], cx_send)
    gone(kv2.at[:, 0], cz_send)
    gone(orecv.at[0:7], o_send)


def solution(mesh):
    n_tm, n_rows = mesh.shape["tm"], mesh.shape["rows"]
    bf = jnp.bfloat16
    vm = pltpu.VMEM
    dma = pltpu.SemaphoreType.DMA

    def body(queries, keys, values, window_lists):
        any_ = pl.BlockSpec(memory_space=pl.ANY)
        return pl.pallas_call(
            functools.partial(kernel, n_tm, n_rows),
            out_shape=jax.ShapeDtypeStruct(queries.shape, bf),
            in_specs=[any_, any_, any_, any_],
            out_specs=pl.BlockSpec(memory_space=pltpu.VMEM),
            scratch_shapes=[
                pltpu.SMEM(window_lists.shape[::-1], jnp.int32),
                vm(queries.shape, bf), vm(queries.shape, bf), vm(queries.shape, bf),
                vm((HEADS, COLS, 2, PART, DIM), bf),
                vm((HEADS, COLS, PART, DIM), bf),
                vm((2, 4, 3, 2, TOK, DIM), bf), vm((4, 3, 2, TOK, DIM), bf), vm((4, 3, 2, TOK, DIM), bf),
                vm((2, 2, 2, TOK, DIM), bf),
                vm((2, COLS, TOK, DIM), bf),
                vm((WIN // 2, TOK, 2 * TOK), jnp.float32),
                vm((TOK, DIM), jnp.float32), vm((2, TOK, 2 * DIM), jnp.float32), vm((2, TOK, DIM), jnp.float32),
                vm((2, COLS, TOK, DIM), bf),
                vm((HEADS, COLS, PART, DIM), bf),
                dma((4,)), dma, dma((COLS, 8)), dma, dma, dma, dma((COLS, 2)), dma, dma((COLS, 2)),
                dma, dma((COLS, 2)), dma, dma((2, 2)), dma, dma((COLS,)), dma((COLS + 2,)),
            ],
            compiler_params=pltpu.CompilerParams(
                collective_id=0, has_side_effects=True, vmem_limit_bytes=53 * 1024 * 1024
            ),
        )(queries, keys, values, window_lists.T)

    row = P("tm", "rows", None, None)
    return jax.shard_map(body, mesh=mesh, in_specs=(row, row, row, P()), out_specs=row, check_vma=False)
```

```python
import functools

import jax
import jax.numpy as jnp
from jax import lax
from jax.experimental import pallas as pl
from jax.experimental.pallas import tpu as pltpu
from jax.sharding import PartitionSpec as P

HEADS = 8
COLS = 4
WIN = 12
TOK = 384
PART = 96
DIM = 128
LOG2E = 1.4426950408889634


def rc(src, dst, ss, rs, dev):
    return pltpu.make_async_remote_copy(
        src_ref=src, dst_ref=dst, send_sem=ss, recv_sem=rs, device_id=dev, device_id_type=pl.DeviceIdType.MESH
    )


def kernel(
    n_tm, n_rows, q_hbm, k_hbm, v_hbm, lists_hbm, out_ref,
    lists, qin, kin, vin, skv, sq, kv01, kv2, kv3, far2, qb, scores, peak, held, held_peak, ob, orecv,
    in_sem, kv_send, kv_recv, q_send, q_recv, z_send, z_recv, x_send, x_recv,
    cx_send, cx_recv, cz_send, cz_recv, o_send, o_recv, loc_sem,
):
    tm = lax.axis_index("tm")
    rows = lax.axis_index("rows")
    x, yh = tm // 2, tm % 2
    z, part = rows // 4, rows % 4
    me = yh * 4 + part

    def member(p):
        return (x * 2 + p // 4, z * 4 + p % 4)

    z_up = (tm, (rows + 4) % n_rows)
    z_dn = (tm, (rows + n_rows - 4) % n_rows)
    x_up = ((tm + 2) % n_tm, rows)
    x_dn = ((tm + n_tm - 2) % n_tm, rows)

    loads = [
        pltpu.make_async_copy(src, dst, in_sem.at[i])
        for i, (src, dst) in enumerate(((k_hbm, kin), (v_hbm, vin), (q_hbm, qin), (lists_hbm, lists)))
    ]
    for c in loads:
        c.start()

    barrier = pltpu.get_barrier_semaphore()

    def greet(d, carry):
        pl.semaphore_signal(barrier, inc=1, device_id=member((me + d) % 8), device_id_type=pl.DeviceIdType.MESH)
        return carry

    lax.fori_loop(1, 8, greet, 0)
    for dev in (z_up, z_dn, x_up, x_dn):
        pl.semaphore_signal(barrier, inc=1, device_id=dev, device_id_type=pl.DeviceIdType.MESH)
    pl.semaphore_wait(barrier, 11)

    def pack(src, ct, p):
        feats = pl.ds(pl.multiple_of(p * DIM, DIM), DIM)
        pieces = []
        for f in range(2):
            for r in range(2):
                full = src[f, r, :, feats].astype(jnp.float32)
                pieces.append(full[ct * 24 : ct * 24 + 24])
        return jnp.concatenate(pieces, axis=0).astype(jnp.bfloat16)

    def rows_of(p):
        return pl.ds(pl.multiple_of((p % 4) * PART, PART), PART)

    my_rows = rows_of(me)

    def tile(ct, layer, row):
        if ct == 2 and not hasattr(layer, "dtype") and layer in (0, 3) and row != 1:
            return far2.at[layer // 3, row // 2]
        return kv01.at[ct, layer, row] if ct < 2 else (kv2, kv3)[ct - 2].at[layer, row]

    def kv_piece(ct, p, source):
        return rc(
            skv.at[p, ct], tile(ct, 1 + source // 4, 1).at[:, rows_of(source)],
            kv_send, kv_recv.at[ct, source], member(p),
        )

    def q_piece(p, source):
        return rc(
            sq.at[p], qb.at[source // 4, :, rows_of(source)], q_send, q_recv, member(p)
        )

    def z_piece(ct, up, p, packed=False):
        return rc(
            skv.at[p, ct] if packed else tile(ct, 1 + p // 4, 1).at[:, rows_of(p)],
            tile(ct, 1 + p // 4, 0 if up else 2).at[:, rows_of(p)],
            z_send, z_recv.at[ct, up], z_up if up else z_dn,
        )

    def x_piece(ct, p, packed=False):
        late = p // 4
        dev = ((tm + 2 * late + n_tm - 2 * (1 - late)) % n_tm, rows)
        return rc(
            skv.at[p, ct] if packed else tile(ct, 1 + late, 1).at[:, rows_of(p)],
            tile(ct, 3 - 3 * late, 1).at[:, rows_of(p)],
            x_send, x_recv.at[ct, late], dev,
        )

    def x_corner(ct, up, row):
        return rc(
            tile(ct, 2 if up else 1, row), tile(ct, 0 if up else 3, row),
            cx_send, cx_recv.at[ct, up], x_up if up else x_dn,
        )

    def z_corner(ct, up):
        layer = 3 if up else 0
        return rc(
            tile(ct, layer, 1), tile(ct, layer, 0 if up else 2),
            cz_send, cz_recv.at[ct - 2, up], z_up if up else z_dn,
        )

    def x_corners(ct):
        return [x_corner(ct, up, row) for up, row in (((1, 0), (0, 2), (1, 2), (0, 0)) if ct < 2 else ((1, 0), (0, 2)))]

    def z_corners(ct):
        return [z_corner(ct, up) for up in (1, 0)]

    def own_copy(ct):
        return pltpu.make_async_copy(skv.at[me, ct], tile(ct, 1 + yh, 1).at[:, my_rows], loc_sem.at[ct])

    def each(first, f):
        def step(d, carry):
            d = d // 2 + 4 * (d % 2)
            f((me + d) % 8, d)
            return carry

        lax.fori_loop(first, 8, step, 0)

    def own_first(ct):
        skv[me, ct, 0] = pack(kin, ct, me)
        skv[me, ct, 1] = pack(vin, ct, me)
        own_copy(ct).start()
        for c in (z_piece(ct, 1, me, True), z_piece(ct, 0, me, True), x_piece(ct, me, True)):
            c.start()

    def send_kv(ct):
        def one(p):
            skv[p, ct, 0] = pack(kin, ct, p)
            skv[p, ct, 1] = pack(vin, ct, p)
            kv_piece(ct, p, me).start()

        return one

    def forward_z(ct, x_too, following=None):
        own_copy(ct).wait()

        def one(partner, d):
            p = (me + 8 - d) % 8
            kv_piece(ct, p, p).wait_recv()
            z_piece(ct, 1, p).start()
            z_piece(ct, 0, p).start()
            if x_too:
                x_piece(ct, p).start()
            if following is not None:
                following(partner)

        each(1, one)

    def forward_x(ct):
        each(1, lambda p, d: x_piece(ct, p).start())

    def landed(ref, sem):
        rc(ref, ref, kv_send, sem, z_up).wait_recv()

    def gone(ref, sem):
        rc(ref, ref, sem, q_recv, z_up).wait_send()

    def block(ct):
        return kv01.at[ct] if ct < 2 else (kv2, kv3)[ct - 2]

    def arrived_z(ct):
        for up in (1, 0):
            landed(block(ct).at[1:3, 0 if up else 2], z_recv.at[ct, up])

    def arrived_x(ct):
        for late in (1, 0):
            landed(tile(ct, 3 - 3 * late, 1), x_recv.at[ct, late])

    def arrived_x_corners(ct):
        for up in (1, 0):
            landed(kv01.at[0, 0 if up else 3, 0 : (2 if ct < 2 else 1)], cx_recv.at[ct, up])

    def begin(copies):
        for c in copies:
            c.start()

    def arrived(copies):
        for c in copies:
            c.wait_recv()

    scale = DIM ** -0.5 * LOG2E

    def o_piece(layer, ct, s):
        p = layer * 4 + s
        return rc(
            ob.at[layer, ct, pl.ds(s * PART, PART)], orecv.at[me, ct], o_send, o_recv.at[ct], member(p)
        )

    def own_o(ct):
        return pltpu.make_async_copy(ob.at[yh, ct, my_rows], orecv.at[me, ct], loc_sem.at[COLS + 1])

    def attend(layer, ct, reach):
        tile_id = ((2 * x + layer) * 8 + z) * COLS + ct

        def place(slot):
            listed = lists[slot, tile_id]
            present = listed >= 0
            if reach == 2:
                f_layer, f_row, f_col = listed // 32, (listed // 4) % 8, listed % 4
                present = present & ~far(f_col, f_layer - 2 * x + 1, f_row - z + 1)
            t = jnp.where(present, listed, tile_id)
            t_layer, t_row, t_col = t // 32, (t // 4) % 8, t % 4
            return t_col, jnp.clip(t_layer - 2 * x + 1, 0, 3), jnp.clip(t_row - z + 1, 0, 2), jnp.where(present, 1.0, 0.0)

        def pick(c_, l_, r_, which):
            found = kv2[l_, r_, which] if reach == 4 else kv01[jnp.clip(c_, 0, 1), l_, r_, which]
            if 1 < reach < 4:
                found = jnp.where(c_ == 2, kv2[l_, r_, which], found)
            if reach > 2:
                found = jnp.where(c_ == 3, kv3[l_, r_, which], found)
                found = jnp.where(far(c_, l_, r_), far2[l_ // 3, r_ // 2, which], found)
            return found

        def far(c_, l_, r_):
            return (c_ == 2) & ((l_ == 0) | (l_ == 3)) & (r_ != 1)

        @pl.when(tm >= 0)
        def _():
            q = qb[layer, ct]
            high = jnp.full((TOK, DIM), -jnp.inf, jnp.float32)
            for j in range(WIN // 2):
                keys = []
                for slot in (2 * j, 2 * j + 1):
                    c_, l_, r_, _ = place(slot)
                    keys.append(pick(c_, l_, r_, 0))
                s = lax.dot_general(
                    q, jnp.concatenate(keys, axis=0), (((1,), (1,)), ((), ())), preferred_element_type=jnp.float32
                )
                scores[j] = s
                for b in range(2 * TOK // DIM):
                    high = jnp.maximum(high, s[:, b * DIM : (b + 1) * DIM])
            peak[...] = jnp.broadcast_to(jnp.max(high, axis=1, keepdims=True) * scale, (TOK, DIM))

        @pl.when(rows >= 0)
        def _():
            top = jnp.concatenate([peak[...]] * (2 * TOK // DIM), axis=1)
            acc = jnp.zeros((TOK, 2 * DIM), jnp.float32)
            for j in range(WIN // 2):
                vals = []
                for slot in (2 * j, 2 * j + 1):
                    c_, l_, r_, flag = place(slot)
                    flag = jnp.full((TOK, DIM), flag, jnp.float32).astype(jnp.bfloat16)
                    vals.append(jnp.concatenate((pick(c_, l_, r_, 1) * flag, flag), axis=1))
                w = jnp.exp2(scores[j] * scale - top).astype(jnp.bfloat16)
                acc = acc + jnp.dot(w, jnp.concatenate(vals, axis=0), preferred_element_type=jnp.float32)
            if reach == 2:
                held[layer] = acc
                held_peak[layer] = peak[...]
            else:
                ob[layer, ct] = (acc[:, :DIM] / acc[:, DIM:]).astype(jnp.bfloat16)

    def attend_far(layer, ct):
        tile_id = ((2 * x + layer) * 8 + z) * COLS + ct
        there = []
        for row in (-1, 1):
            corner = ((2 * x - 1 + 3 * layer) * 8 + z + row) * COLS + 2
            hits = [jnp.where(lists[slot, tile_id] == corner, 1.0, 0.0) for slot in range(WIN)]
            there.append(functools.reduce(jnp.maximum, hits))

        @pl.when(tm >= 0)
        def _():
            keys = jnp.concatenate([far2[layer, row, 0] for row in (0, 1)], axis=0)
            s = lax.dot_general(
                qb[layer, ct], keys, (((1,), (1,)), ((), ())), preferred_element_type=jnp.float32
            )
            high = jnp.full((TOK, DIM), -1e30, jnp.float32)
            for row in range(2):
                part_s = s[:, row * TOK : (row + 1) * TOK] + (there[row] - 1.0) * 1e30
                scores[0, :, row * TOK : (row + 1) * TOK] = part_s
                for b in range(TOK // DIM):
                    high = jnp.maximum(high, part_s[:, b * DIM : (b + 1) * DIM])
            peak[...] = jnp.maximum(
                held_peak[layer], jnp.broadcast_to(jnp.max(high, axis=1, keepdims=True) * scale, (TOK, DIM))
            )

        @pl.when(rows >= 0)
        def _():
            top = jnp.concatenate([peak[...]] * (2 * TOK // DIM), axis=1)
            vals = []
            for row in range(2):
                flag = jnp.full((TOK, DIM), there[row], jnp.float32).astype(jnp.bfloat16)
                vals.append(jnp.concatenate((far2[layer, row, 1] * flag, flag), axis=1))
            w = jnp.exp2(scores[0] * scale - top).astype(jnp.bfloat16)
            keep = jnp.exp2(held_peak[layer] - peak[...])
            acc = held[layer] * jnp.concatenate((keep, keep), axis=1) + jnp.dot(
                w, jnp.concatenate(vals, axis=0), preferred_element_type=jnp.float32
            )
            ob[layer, ct] = (acc[:, :DIM] / acc[:, DIM:]).astype(jnp.bfloat16)

    def hold(layer, carry):
        attend(layer, 1, 2)
        return carry

    def finish(first, count, work):
        def step(i, carry):
            layer, ct = i % 2, first + i // 2
            work(layer, ct)
            for s in range(4):
                @pl.when(layer * 4 + s != me)
                def _():
                    o_piece(layer, ct, s).start()

            @pl.when(layer == yh)
            def _():
                own_o(ct).start()

            return carry

        lax.fori_loop(0, 2 * count, step, 0)

    def own_q():
        return pltpu.make_async_copy(sq.at[me], qb.at[yh, :, my_rows], loc_sem.at[COLS])

    def pack_q(p):
        for ct in range(COLS):
            sq[p, ct] = pack(qin, ct, p)

    def send_q(p):
        pack_q(p)
        q_piece(p, me).start()

    loads[0].wait()
    loads[1].wait()
    own_first(0)
    each(1, lambda p, d: send_kv(0)(p))
    own_first(1)
    forward_z(0, True, send_kv(1))
    own_first(2)
    forward_z(1, True, send_kv(2))
    arrived_z(0)
    begin(x_corners(0))
    own_first(3)
    forward_z(2, False, send_kv(3))
    loads[2].wait()
    each(1, lambda p, d: send_q(p))
    pack_q(me)
    own_q().start()
    arrived_z(1)
    begin(x_corners(1))
    forward_x(2)
    forward_z(3, True)
    arrived_z(2)
    begin(x_corners(2))
    own_q().wait()
    loads[3].wait()
    landed(sq.at[0:7], q_recv)
    for ct in (0, 1):
        arrived_x(ct)
        arrived_x_corners(ct)
    finish(0, 1, lambda layer, ct: attend(layer, ct, 1))
    arrived_x(2)
    begin(z_corners(2))
    arrived_z(3)
    begin(x_corners(3))
    arrived_x(3)
    begin(z_corners(3))
    lax.fori_loop(0, 2, hold, 0)
    arrived_x_corners(2)
    arrived(z_corners(2))
    finish(1, 1, attend_far)
    arrived_x_corners(3)
    arrived(z_corners(3))
    finish(2, 1, lambda layer, ct: attend(layer, ct, 3))
    finish(3, 1, lambda layer, ct: attend(layer, ct, 4))

    pltpu.make_async_copy(orecv.at[me], orecv.at[me], loc_sem.at[COLS + 1]).wait()
    for ct in range(COLS):
        landed(orecv.at[0:7, ct], o_recv.at[ct])

    for h in range(HEADS):
        parts = [orecv[h, ct].astype(jnp.float32) for ct in range(COLS)]
        for f in range(2):
            for r in range(2):
                n = (2 * f + r) * 24
                row = jnp.concatenate([p_[n : n + 24] for p_ in parts], axis=0)
                out_ref[f, r, :, h * DIM : (h + 1) * DIM] = row.astype(jnp.bfloat16)

    gone(skv.at[0:7], kv_send)
    gone(sq.at[0:7], q_send)
    gone(kv01.at[:, :, 0:2], z_send)
    gone(kv2.at[:, 0:2], x_send)
    gone(kv01.at[0], cx_send)
    gone(kv2.at[:, 0], cz_send)
    gone(orecv.at[0:7], o_send)


def solution(mesh):
    n_tm, n_rows = mesh.shape["tm"], mesh.shape["rows"]
    bf = jnp.bfloat16
    vm = pltpu.VMEM
    dma = pltpu.SemaphoreType.DMA

    def body(queries, keys, values, window_lists):
        any_ = pl.BlockSpec(memory_space=pl.ANY)
        return pl.pallas_call(
            functools.partial(kernel, n_tm, n_rows),
            out_shape=jax.ShapeDtypeStruct(queries.shape, bf),
            in_specs=[any_, any_, any_, any_],
            out_specs=pl.BlockSpec(memory_space=pltpu.VMEM),
            scratch_shapes=[
                pltpu.SMEM(window_lists.shape[::-1], jnp.int32),
                vm(queries.shape, bf), vm(queries.shape, bf), vm(queries.shape, bf),
                vm((HEADS, COLS, 2, PART, DIM), bf),
                vm((HEADS, COLS, PART, DIM), bf),
                vm((2, 4, 3, 2, TOK, DIM), bf), vm((4, 3, 2, TOK, DIM), bf), vm((4, 3, 2, TOK, DIM), bf),
                vm((2, 2, 2, TOK, DIM), bf),
                vm((2, COLS, TOK, DIM), bf),
                vm((WIN // 2, TOK, 2 * TOK), jnp.float32),
                vm((TOK, DIM), jnp.float32), vm((2, TOK, 2 * DIM), jnp.float32), vm((2, TOK, DIM), jnp.float32),
                vm((2, COLS, TOK, DIM), bf),
                vm((HEADS, COLS, PART, DIM), bf),
                dma((4,)), dma, dma((COLS, 8)), dma, dma, dma, dma((COLS, 2)), dma, dma((COLS, 2)),
                dma, dma((COLS, 2)), dma, dma((2, 2)), dma, dma((COLS,)), dma((COLS + 2,)),
            ],
            compiler_params=pltpu.CompilerParams(
                collective_id=0, has_side_effects=True, vmem_limit_bytes=53 * 1024 * 1024
            ),
        )(queries, keys, values, window_lists.T)

    row = P("tm", "rows", None, None)
    return jax.shard_map(body, mesh=mesh, in_specs=(row, row, row, P()), out_specs=row, check_vma=False)
```

```python
import functools

import jax
import jax.numpy as jnp
from jax import lax
from jax.experimental import pallas as pl
from jax.experimental.pallas import tpu as pltpu
from jax.sharding import PartitionSpec as P

HEADS = 8
COLS = 4
WIN = 12
TOK = 384
PART = 96
DIM = 128
LOG2E = 1.4426950408889634


def rc(src, dst, ss, rs, dev):
    return pltpu.make_async_remote_copy(
        src_ref=src, dst_ref=dst, send_sem=ss, recv_sem=rs, device_id=dev, device_id_type=pl.DeviceIdType.MESH
    )


def kernel(
    n_tm, n_rows, q_hbm, k_hbm, v_hbm, lists_hbm, out_ref,
    lists, qin, kin, vin, skv, sq, kv01, kv2, kv3, far2, qb, scores, peak, held, held_peak, ob, orecv,
    in_sem, kv_send, kv_recv, q_send, q_recv, z_send, z_recv, x_send, x_recv,
    cx_send, cx_recv, cz_send, cz_recv, o_send, o_recv, loc_sem,
):
    tm = lax.axis_index("tm")
    rows = lax.axis_index("rows")
    x, yh = tm // 2, tm % 2
    z, part = rows // 4, rows % 4
    me = yh * 4 + part

    def member(p):
        return (x * 2 + p // 4, z * 4 + p % 4)

    z_up = (tm, (rows + 4) % n_rows)
    z_dn = (tm, (rows + n_rows - 4) % n_rows)
    x_up = ((tm + 2) % n_tm, rows)
    x_dn = ((tm + n_tm - 2) % n_tm, rows)

    halves = [(k_hbm, kin, 0), (v_hbm, vin, 0), (k_hbm, kin, 48), (v_hbm, vin, 48)]
    loads = [
        pltpu.make_async_copy(src.at[:, :, w : w + 48], dst.at[:, :, w : w + 48], in_sem.at[i])
        for i, (src, dst, w) in enumerate(halves)
    ] + [pltpu.make_async_copy(q_hbm, qin, in_sem.at[4]), pltpu.make_async_copy(lists_hbm, lists, in_sem.at[5])]
    for c in loads:
        c.start()

    barrier = pltpu.get_barrier_semaphore()

    def greet(d, carry):
        pl.semaphore_signal(barrier, inc=1, device_id=member((me + d) % 8), device_id_type=pl.DeviceIdType.MESH)
        return carry

    lax.fori_loop(1, 8, greet, 0)
    for dev in (z_up, z_dn, x_up, x_dn):
        pl.semaphore_signal(barrier, inc=1, device_id=dev, device_id_type=pl.DeviceIdType.MESH)
    pl.semaphore_wait(barrier, 11)

    def pack(src, ct, p):
        feats = pl.ds(pl.multiple_of(p * DIM, DIM), DIM)
        pieces = []
        for f in range(2):
            for r in range(2):
                half = src[f, r, ct // 2 * 48 : ct // 2 * 48 + 48, feats].astype(jnp.float32)
                pieces.append(half[ct % 2 * 24 : ct % 2 * 24 + 24])
        return jnp.concatenate(pieces, axis=0).astype(jnp.bfloat16)

    def rows_of(p):
        return pl.ds(pl.multiple_of((p % 4) * PART, PART), PART)

    my_rows = rows_of(me)

    def tile(ct, layer, row):
        if ct == 2 and not hasattr(layer, "dtype") and layer in (0, 3) and row != 1:
            return far2.at[layer // 3, row // 2]
        return kv01.at[ct, layer, row] if ct < 2 else (kv2, kv3)[ct - 2].at[layer, row]

    def kv_piece(ct, p, source):
        return rc(
            skv.at[p, ct], tile(ct, 1 + source // 4, 1).at[:, rows_of(source)],
            kv_send, kv_recv.at[ct, source], member(p),
        )

    def q_piece(p, source):
        return rc(
            sq.at[p], qb.at[source // 4, :, rows_of(source)], q_send, q_recv, member(p)
        )

    def z_piece(ct, up, p, packed=False):
        return rc(
            skv.at[p, ct] if packed else tile(ct, 1 + p // 4, 1).at[:, rows_of(p)],
            tile(ct, 1 + p // 4, 0 if up else 2).at[:, rows_of(p)],
            z_send, z_recv.at[ct, up], z_up if up else z_dn,
        )

    def x_piece(ct, p, packed=False):
        late = p // 4
        dev = ((tm + 2 * late + n_tm - 2 * (1 - late)) % n_tm, rows)
        return rc(
            skv.at[p, ct] if packed else tile(ct, 1 + late, 1).at[:, rows_of(p)],
            tile(ct, 3 - 3 * late, 1).at[:, rows_of(p)],
            x_send, x_recv.at[ct, late], dev,
        )

    def x_corner(ct, up, row):
        return rc(
            tile(ct, 2 if up else 1, row), tile(ct, 0 if up else 3, row),
            cx_send, cx_recv.at[ct, up], x_up if up else x_dn,
        )

    def z_corner(ct, up):
        layer = 3 if up else 0
        return rc(
            tile(ct, layer, 1), tile(ct, layer, 0 if up else 2),
            cz_send, cz_recv.at[ct - 2, up], z_up if up else z_dn,
        )

    def x_corners(ct):
        return [x_corner(ct, up, row) for up, row in (((1, 0), (0, 2), (1, 2), (0, 0)) if ct < 2 else ((1, 0), (0, 2)))]

    def z_corners(ct):
        return [z_corner(ct, up) for up in (1, 0)]

    def own_copy(ct):
        return pltpu.make_async_copy(skv.at[me, ct], tile(ct, 1 + yh, 1).at[:, my_rows], loc_sem.at[ct])

    def each(first, f):
        def step(d, carry):
            d = d // 2 + 4 * (d % 2)
            f((me + d) % 8, d)
            return carry

        lax.fori_loop(first, 8, step, 0)

    def own_first(ct):
        skv[me, ct, 0] = pack(kin, ct, me)
        skv[me, ct, 1] = pack(vin, ct, me)
        own_copy(ct).start()
        for c in (z_piece(ct, 1, me, True), z_piece(ct, 0, me, True), x_piece(ct, me, True)):
            c.start()

    def send_kv(ct):
        def one(p):
            skv[p, ct, 0] = pack(kin, ct, p)
            skv[p, ct, 1] = pack(vin, ct, p)
            kv_piece(ct, p, me).start()

        return one

    def forward_z(ct, x_too, following=None):
        own_copy(ct).wait()

        def one(partner, d):
            p = (me + 8 - d) % 8
            kv_piece(ct, p, p).wait_recv()
            z_piece(ct, 1, p).start()
            z_piece(ct, 0, p).start()
            if x_too:
                x_piece(ct, p).start()
            if following is not None:
                following(partner)

        each(1, one)

    def forward_x(ct):
        each(1, lambda p, d: x_piece(ct, p).start())

    def landed(ref, sem):
        rc(ref, ref, kv_send, sem, z_up).wait_recv()

    def gone(ref, sem):
        rc(ref, ref, sem, q_recv, z_up).wait_send()

    def block(ct):
        return kv01.at[ct] if ct < 2 else (kv2, kv3)[ct - 2]

    def arrived_z(ct):
        for up in (1, 0):
            landed(block(ct).at[1:3, 0 if up else 2], z_recv.at[ct, up])

    def arrived_x(ct):
        for late in (1, 0):
            landed(tile(ct, 3 - 3 * late, 1), x_recv.at[ct, late])

    def arrived_x_corners(ct):
        for up in (1, 0):
            landed(kv01.at[0, 0 if up else 3, 0 : (2 if ct < 2 else 1)], cx_recv.at[ct, up])

    def begin(copies):
        for c in copies:
            c.start()

    def arrived(copies):
        for c in copies:
            c.wait_recv()

    scale = DIM ** -0.5 * LOG2E

    def o_piece(layer, ct, s):
        p = layer * 4 + s
        return rc(
            ob.at[layer, ct, pl.ds(s * PART, PART)], orecv.at[me, ct], o_send, o_recv.at[ct], member(p)
        )

    def own_o(ct):
        return pltpu.make_async_copy(ob.at[yh, ct, my_rows], orecv.at[me, ct], loc_sem.at[COLS + 1])

    def attend(layer, ct, reach):
        tile_id = ((2 * x + layer) * 8 + z) * COLS + ct

        def place(slot):
            listed = lists[slot, tile_id]
            present = listed >= 0
            if reach == 2:
                f_layer, f_row, f_col = listed // 32, (listed // 4) % 8, listed % 4
                present = present & ~far(f_col, f_layer - 2 * x + 1, f_row - z + 1)
            t = jnp.where(present, listed, tile_id)
            t_layer, t_row, t_col = t // 32, (t // 4) % 8, t % 4
            return t_col, jnp.clip(t_layer - 2 * x + 1, 0, 3), jnp.clip(t_row - z + 1, 0, 2), jnp.where(present, 1.0, 0.0)

        def pick(c_, l_, r_, which):
            found = kv2[l_, r_, which] if reach == 4 else kv01[jnp.clip(c_, 0, 1), l_, r_, which]
            if 1 < reach < 4:
                found = jnp.where(c_ == 2, kv2[l_, r_, which], found)
            if reach > 2:
                found = jnp.where(c_ == 3, kv3[l_, r_, which], found)
                found = jnp.where(far(c_, l_, r_), far2[l_ // 3, r_ // 2, which], found)
            return found

        def far(c_, l_, r_):
            return (c_ == 2) & ((l_ == 0) | (l_ == 3)) & (r_ != 1)

        @pl.when(tm >= 0)
        def _():
            q = qb[layer, ct]
            high = jnp.full((TOK, DIM), -jnp.inf, jnp.float32)
            for j in range(WIN // 2):
                keys = []
                for slot in (2 * j, 2 * j + 1):
                    c_, l_, r_, _ = place(slot)
                    keys.append(pick(c_, l_, r_, 0))
                s = lax.dot_general(
                    q, jnp.concatenate(keys, axis=0), (((1,), (1,)), ((), ())), preferred_element_type=jnp.float32
                )
                scores[j] = s
                for b in range(2 * TOK // DIM):
                    high = jnp.maximum(high, s[:, b * DIM : (b + 1) * DIM])
            peak[...] = jnp.broadcast_to(jnp.max(high, axis=1, keepdims=True) * scale, (TOK, DIM))

        @pl.when(rows >= 0)
        def _():
            top = jnp.concatenate([peak[...]] * (2 * TOK // DIM), axis=1)
            acc = jnp.zeros((TOK, 2 * DIM), jnp.float32)
            for j in range(WIN // 2):
                vals = []
                for slot in (2 * j, 2 * j + 1):
                    c_, l_, r_, flag = place(slot)
                    flag = jnp.full((TOK, DIM), flag, jnp.float32).astype(jnp.bfloat16)
                    vals.append(jnp.concatenate((pick(c_, l_, r_, 1) * flag, flag), axis=1))
                w = jnp.exp2(scores[j] * scale - top).astype(jnp.bfloat16)
                acc = acc + jnp.dot(w, jnp.concatenate(vals, axis=0), preferred_element_type=jnp.float32)
            if reach == 2:
                held[layer] = acc
                held_peak[layer] = peak[...]
            else:
                ob[layer, ct] = (acc[:, :DIM] / acc[:, DIM:]).astype(jnp.bfloat16)

    def attend_far(layer, ct):
        tile_id = ((2 * x + layer) * 8 + z) * COLS + ct
        there = []
        for row in (-1, 1):
            corner = ((2 * x - 1 + 3 * layer) * 8 + z + row) * COLS + 2
            hits = [jnp.where(lists[slot, tile_id] == corner, 1.0, 0.0) for slot in range(WIN)]
            there.append(functools.reduce(jnp.maximum, hits))

        @pl.when(tm >= 0)
        def _():
            keys = jnp.concatenate([far2[layer, row, 0] for row in (0, 1)], axis=0)
            s = lax.dot_general(
                qb[layer, ct], keys, (((1,), (1,)), ((), ())), preferred_element_type=jnp.float32
            )
            high = jnp.full((TOK, DIM), -1e30, jnp.float32)
            for row in range(2):
                part_s = s[:, row * TOK : (row + 1) * TOK] + (there[row] - 1.0) * 1e30
                scores[0, :, row * TOK : (row + 1) * TOK] = part_s
                for b in range(TOK // DIM):
                    high = jnp.maximum(high, part_s[:, b * DIM : (b + 1) * DIM])
            peak[...] = jnp.maximum(
                held_peak[layer], jnp.broadcast_to(jnp.max(high, axis=1, keepdims=True) * scale, (TOK, DIM))
            )

        @pl.when(rows >= 0)
        def _():
            top = jnp.concatenate([peak[...]] * (2 * TOK // DIM), axis=1)
            vals = []
            for row in range(2):
                flag = jnp.full((TOK, DIM), there[row], jnp.float32).astype(jnp.bfloat16)
                vals.append(jnp.concatenate((far2[layer, row, 1] * flag, flag), axis=1))
            w = jnp.exp2(scores[0] * scale - top).astype(jnp.bfloat16)
            keep = jnp.exp2(held_peak[layer] - peak[...])
            acc = held[layer] * jnp.concatenate((keep, keep), axis=1) + jnp.dot(
                w, jnp.concatenate(vals, axis=0), preferred_element_type=jnp.float32
            )
            ob[layer, ct] = (acc[:, :DIM] / acc[:, DIM:]).astype(jnp.bfloat16)

    def hold(layer, carry):
        attend(layer, 1, 2)
        return carry

    def finish(first, count, work):
        def step(i, carry):
            layer, ct = i % 2, first + i // 2
            work(layer, ct)
            for s in range(4):
                @pl.when(layer * 4 + s != me)
                def _():
                    o_piece(layer, ct, s).start()

            @pl.when(layer == yh)
            def _():
                own_o(ct).start()

            return carry

        lax.fori_loop(0, 2 * count, step, 0)

    def own_q():
        return pltpu.make_async_copy(sq.at[me], qb.at[yh, :, my_rows], loc_sem.at[COLS])

    def pack_q(p):
        for ct in range(COLS):
            sq[p, ct] = pack(qin, ct, p)

    def send_q(p):
        pack_q(p)
        q_piece(p, me).start()

    loads[0].wait()
    loads[1].wait()
    own_first(0)
    each(1, lambda p, d: send_kv(0)(p))
    own_first(1)
    forward_z(0, True, send_kv(1))
    loads[2].wait()
    loads[3].wait()
    own_first(2)
    forward_z(1, True, send_kv(2))
    arrived_z(0)
    begin(x_corners(0))
    own_first(3)
    forward_z(2, False, send_kv(3))
    loads[4].wait()
    each(1, lambda p, d: send_q(p))
    pack_q(me)
    own_q().start()
    arrived_z(1)
    begin(x_corners(1))
    forward_x(2)
    forward_z(3, True)
    arrived_z(2)
    begin(x_corners(2))
    own_q().wait()
    loads[5].wait()
    landed(sq.at[0:7], q_recv)
    for ct in (0, 1):
        arrived_x(ct)
        arrived_x_corners(ct)
    finish(0, 1, lambda layer, ct: attend(layer, ct, 1))
    arrived_x(2)
    begin(z_corners(2))
    arrived_z(3)
    begin(x_corners(3))
    arrived_x(3)
    begin(z_corners(3))
    lax.fori_loop(0, 2, hold, 0)
    arrived_x_corners(2)
    arrived(z_corners(2))
    finish(1, 1, attend_far)
    arrived_x_corners(3)
    arrived(z_corners(3))
    finish(2, 1, lambda layer, ct: attend(layer, ct, 3))
    finish(3, 1, lambda layer, ct: attend(layer, ct, 4))

    pltpu.make_async_copy(orecv.at[me], orecv.at[me], loc_sem.at[COLS + 1]).wait()
    for ct in range(COLS):
        landed(orecv.at[0:7, ct], o_recv.at[ct])

    for h in range(HEADS):
        parts = [orecv[h, ct].astype(jnp.float32) for ct in range(COLS)]
        for f in range(2):
            for r in range(2):
                n = (2 * f + r) * 24
                row = jnp.concatenate([p_[n : n + 24] for p_ in parts], axis=0)
                out_ref[f, r, :, h * DIM : (h + 1) * DIM] = row.astype(jnp.bfloat16)

    gone(skv.at[0:7], kv_send)
    gone(sq.at[0:7], q_send)
    gone(kv01.at[:, :, 0:2], z_send)
    gone(kv2.at[:, 0:2], x_send)
    gone(kv01.at[0], cx_send)
    gone(kv2.at[:, 0], cz_send)
    gone(orecv.at[0:7], o_send)


def solution(mesh):
    n_tm, n_rows = mesh.shape["tm"], mesh.shape["rows"]
    bf = jnp.bfloat16
    vm = pltpu.VMEM
    dma = pltpu.SemaphoreType.DMA

    def body(queries, keys, values, window_lists):
        any_ = pl.BlockSpec(memory_space=pl.ANY)
        return pl.pallas_call(
            functools.partial(kernel, n_tm, n_rows),
            out_shape=jax.ShapeDtypeStruct(queries.shape, bf),
            in_specs=[any_, any_, any_, any_],
            out_specs=pl.BlockSpec(memory_space=pltpu.VMEM),
            scratch_shapes=[
                pltpu.SMEM(window_lists.shape[::-1], jnp.int32),
                vm(queries.shape, bf), vm(queries.shape, bf), vm(queries.shape, bf),
                vm((HEADS, COLS, 2, PART, DIM), bf),
                vm((HEADS, COLS, PART, DIM), bf),
                vm((2, 4, 3, 2, TOK, DIM), bf), vm((4, 3, 2, TOK, DIM), bf), vm((4, 3, 2, TOK, DIM), bf),
                vm((2, 2, 2, TOK, DIM), bf),
                vm((2, COLS, TOK, DIM), bf),
                vm((WIN // 2, TOK, 2 * TOK), jnp.float32),
                vm((TOK, DIM), jnp.float32), vm((2, TOK, 2 * DIM), jnp.float32), vm((2, TOK, DIM), jnp.float32),
                vm((2, COLS, TOK, DIM), bf),
                vm((HEADS, COLS, PART, DIM), bf),
                dma((6,)), dma, dma((COLS, 8)), dma, dma, dma, dma((COLS, 2)), dma, dma((COLS, 2)),
                dma, dma((COLS, 2)), dma, dma((2, 2)), dma, dma((COLS,)), dma((COLS + 2,)),
            ],
            compiler_params=pltpu.CompilerParams(
                collective_id=0, has_side_effects=True, vmem_limit_bytes=53 * 1024 * 1024
            ),
        )(queries, keys, values, window_lists.T)

    row = P("tm", "rows", None, None)
    return jax.shard_map(body, mesh=mesh, in_specs=(row, row, row, P()), out_specs=row, check_vma=False)
```
